128 devices in a mesh: vrow: 8 (over z, core), ecol: 16 (over x, y).
Axes of the slice: x: 4, y: 4, z: 4, core: 2. Of those that a mesh axis runs over, the one named last changes fastest.
Arguments:
- features: bfloat16 [32768, 256], P(('vrow', 'ecol')), may hold values from -6 to 6
- grad_out: bfloat16 [32768, 256], P(('vrow', 'ecol')), may hold values from -6 to 6
- theta: bfloat16 [256, 256], replicated, may hold values from -0.375 to 0.375
- tile_values: bfloat16 [32768, 128, 128], P(('vrow', 'ecol')), may hold values from -0.09375 to 0.09375
- tile_rows: int32 [32768], P(('vrow', 'ecol')), may hold values from 0 to 31
- tile_cols: int32 [32768], P(('vrow', 'ecol')), may hold values from 0 to 23
- tile_count: int32 [128], P(('vrow', 'ecol')), may hold values from 1 to 256, 12288 in all
- vertex_degree: int32 [32768], P(('vrow', 'ecol')), may hold values from 1 to 8
- edge_weight: float32 [16, 3072], P('ecol', 'vrow'), may hold values from 0.25 to 4
- edge_degree: int32 [16, 3072], P('ecol', 'vrow'), may hold values from 1 to 8
Outputs:
- out_y: bfloat16 [32768, 256], P(('vrow', 'ecol'))
- grad_x: bfloat16 [32768, 256], P(('vrow', 'ecol'))
- grad_theta: float32 [256, 256], replicated
- grad_w: float32 [16, 3072], P('ecol', 'vrow')
The draws below stay inside these ranges and needn't reach their ends.
Inputs may be any that keep to these rules, and one draw needn't show every extreme that they name: `tile_count`: live tile slots of a device; some device has all 256 live.
All inputs are finite; a program needn't handle non-finite values.
Results may differ from the reference program's by a relative error of at most 0.0055.
Values may be sent and summed in bfloat16 or wider, within the bound.
A program may use at most 128 MiB of HBM per device.

```python
import math
import jax
import jax.numpy as jnp
import numpy as np
from jax import lax

F = 256
TILE = 128
VB = 32
EB = 24
TILES_DEV = 256
NV = 32768
EDGES_COL = 3072
TILES = 32768
N_VROW = 8
N_ECOL = 16


def place_ends(drawn, stream_key, least, high):
    longest = drawn.shape.index(max(drawn.shape))
    spots = []
    for shift in (0, 1):
        where = [jax.random.randint(jax.random.fold_in(stream_key, axis), (), 0, length) for axis, length in enumerate(drawn.shape)]
        where[longest] = (where[longest] + shift) % drawn.shape[longest]
        spots.append(tuple(where))
    return drawn.at[spots[0]].set(least).at[spots[1]].set(high)


def shard_levels(key, shape, split, least, high):
    gain = 1.0
    for dim, parts in split:
        heights = jax.random.uniform(jax.random.fold_in(jax.random.fold_in(key, 6), dim), (parts,), jnp.float32, least / len(split), high / len(split))
        gain = gain * jnp.repeat(jnp.exp(heights), shape[dim] // parts).reshape((-1,) + (1,) * (len(shape) - 1 - dim))
    return gain


def rank_bounds(amount, lean):
    weights = [(1 << 20) // math.isqrt(grade ** lean) + 1 for grade in range(1, amount + 1)]
    scale = 1 + sum(weights) // (1 << 30)
    return np.cumsum(np.array([max(1, weight // scale) for weight in weights]))


def ranked(rng, dims, amount, skew):
    table = rank_bounds(amount, skew)
    lot = jax.random.randint(jax.random.fold_in(rng, 1), dims, 0, int(table[amount - 1]))
    standing = jnp.searchsorted(jnp.asarray(table, jnp.int32), lot, side="right")
    return jax.random.permutation(jax.random.fold_in(rng, 2), amount)[standing].astype(jnp.int32)


def length_profile(number_of, total, limit, lean):
    weights = [(1 << 20) // math.isqrt(standing ** lean) + 1 for standing in range(2, number_of + 1)]
    rest, holding = total - limit - (number_of - 1), [1] * (number_of - 1)
    while rest > 0:
        free = [i for i in range(number_of - 1) if holding[i] < limit]
        whole, remaining = sum([weights[i] for i in free]), rest
        for i in free:
            more = min(limit - holding[i], max(1, remaining * weights[i] // whole), rest)
            holding[i] = holding[i] + more
            rest = rest - more
    return np.array([limit] + holding)


def ragged(key, number_of, total, limit, lean):
    if number_of == 2:
        one = jax.random.randint(key, (), max(1, total - limit), min(limit, total - 1) + 1)
        return jnp.stack([one, total - one])
    tallies = jnp.asarray(length_profile(number_of, total, limit, lean), jnp.int32)
    twos = (number_of - 1) // 2
    donor, sink = tallies[1:1 + 2 * twos:2], tallies[2:2 + 2 * twos:2]
    margin = jnp.minimum(donor - 1, limit - sink)
    passed = jax.random.randint(jax.random.fold_in(key, 1), (twos,), 0, 1 << 20) % (margin + 1)
    tallies = tallies.at[1:1 + 2 * twos:2].set(donor - passed).at[2:2 + 2 * twos:2].set(sink + passed)
    return tallies[jax.random.permutation(jax.random.fold_in(key, 2), number_of)]


def normal_values(own_key, dims, deviation, most, shards=(), kind=jnp.bfloat16):
    drawn = jax.random.normal(own_key, dims, jnp.float32) * deviation
    if len(shards) > 0:
        drawn = shard_levels(own_key, dims, shards, -0.22, 0.18) * drawn
    return jnp.clip(drawn, min=-most, max=most).astype(kind)


def setup_inputs(seed: int = 0) -> dict:
    seeds = jax.random.split(jax.random.key(seed), 11)
    return {
        "features": normal_values(seeds[0], (NV, F), 1.0, 6.0, ((0, 128),)),
        "grad_out": normal_values(seeds[1], (NV, F), 1.0, 6.0, ((0, 128),)),
        "theta": normal_values(seeds[2], (F, F), F ** -0.5, 0.375),
        "tile_values": normal_values(seeds[3], (TILES, TILE, TILE), (16 * TILES_DEV) ** -0.5, 0.09375, ((0, 128),)),
        "tile_rows": place_ends(ranked(seeds[4], (TILES,), VB, 2), jax.random.fold_in(seeds[4], 3), 0, VB - 1).astype(jnp.int32),
        "tile_cols": place_ends(jax.random.randint(seeds[5], (TILES,), 0, EB), jax.random.fold_in(seeds[5], 1), 0, EB - 1).astype(jnp.int32),
        "tile_count": ragged(seeds[6], N_VROW * N_ECOL, N_VROW * N_ECOL * TILES_DEV * 3 // 8, TILES_DEV, 2).astype(jnp.int32),
        "vertex_degree": place_ends(jax.random.randint(seeds[7], (NV,), 1, 9), jax.random.fold_in(seeds[7], 1), 1, 8).astype(jnp.int32),
        "edge_weight": jnp.clip(jnp.exp(math.log(4.0) - 2.7725887 * jax.random.uniform(seeds[8], (N_ECOL, EDGES_COL), jnp.float32) ** shard_levels(seeds[8], (N_ECOL, EDGES_COL), ((0, 16), (1, 8)), -0.2, 0.2)), 0.25, 4.0),
        "edge_degree": place_ends(jax.random.randint(seeds[9], (N_ECOL, EDGES_COL), 1, 9), jax.random.fold_in(seeds[9], 1), 1, 8).astype(jnp.int32),
    }


def accumulate(values, rows, cols, live, panels, out_blocks, forward):
    step = math.gcd(32, TILES_DEV)
    tile = values.shape[1]
    width = panels.shape[-1]
    blocks = (live + step - 1) // step

    def turn(index, total):
        first = (index * step).astype(jnp.int32)
        vals = lax.dynamic_slice_in_dim(values, first, step, 0).astype(jnp.float32)
        rws = lax.dynamic_slice_in_dim(rows, first, step, 0)
        cls = lax.dynamic_slice_in_dim(cols, first, step, 0)
        valid = first + jnp.arange(step, dtype=jnp.int32) < live
        if forward:
            picked = panels[rws].astype(jnp.float32)
            product = jnp.einsum('tvc,tvw->tcw', vals, picked)
            target = cls
        else:
            picked = panels[cls].astype(jnp.float32)
            product = jnp.einsum('tvc,tcw->tvw', vals, picked)
            target = rws
        onehot = ((target[None, :] == jnp.arange(out_blocks, dtype=jnp.int32)[:, None]) & valid[None, :]).astype(jnp.float32)
        return total + jnp.einsum('bt,tcw->bcw', onehot, product, precision=lax.Precision.HIGHEST)
    init = jnp.zeros((out_blocks, tile, width), jnp.float32)
    return lax.fori_loop(0, blocks, turn, init)

def reference(features, grad_out, theta, tile_values, tile_rows, tile_cols, tile_count, vertex_degree, edge_weight, edge_degree):
    vertex_scale = 1.0 / jnp.sqrt(vertex_degree.astype(jnp.float32))
    projected = jnp.dot(features, theta, preferred_element_type=jnp.float32)
    scaled_z = (projected * vertex_scale[:, None]).astype(jnp.bfloat16)
    scaled_g = (grad_out.astype(jnp.float32) * vertex_scale[:, None]).astype(jnp.bfloat16)
    stacked = jnp.concatenate([scaled_z, scaled_g], axis=1)
    width = stacked.shape[1]
    panel_rows = VB * TILE
    col_rows = EB * TILE
    devices = N_VROW * N_ECOL

    def device_tiles(device):
        first = (device * TILES_DEV).astype(jnp.int32)
        values = lax.dynamic_slice_in_dim(tile_values, first, TILES_DEV, 0)
        rows = lax.dynamic_slice_in_dim(tile_rows, first, TILES_DEV, 0)
        cols = lax.dynamic_slice_in_dim(tile_cols, first, TILES_DEV, 0)
        return (values, rows, cols, tile_count[device])

    def edge_device(device, sums):
        device = jnp.asarray(device).astype(jnp.int32)
        row_index = device // N_ECOL
        col_index = device % N_ECOL
        values, rows, cols, live = device_tiles(device)
        panels = lax.dynamic_slice_in_dim(stacked, (row_index * panel_rows).astype(jnp.int32), panel_rows, 0).reshape(VB, TILE, width)
        part = accumulate(values, rows, cols, live, panels, EB, True).reshape(1, col_rows, width)
        current = lax.dynamic_slice_in_dim(sums, col_index, 1, 0)
        return lax.dynamic_update_slice_in_dim(sums, current + part, col_index, 0)
    sums = lax.fori_loop(0, devices, edge_device, jnp.zeros((N_ECOL, col_rows, width), jnp.float32))
    degree_edge = edge_degree.astype(jnp.float32)
    coefs = edge_weight / degree_edge
    spread = (sums * coefs[:, :, None]).astype(jnp.bfloat16)
    grad_w = lax.optimization_barrier(jnp.sum(sums[:, :, :F] * sums[:, :, F:], axis=2)) / degree_edge

    def vertex_device(device, total):
        device = jnp.asarray(device).astype(jnp.int32)
        row_index = device // N_ECOL
        col_index = device % N_ECOL
        values, rows, cols, live = device_tiles(device)
        panels = lax.dynamic_slice_in_dim(spread, col_index, 1, 0).reshape(EB, TILE, width)
        part = accumulate(values, rows, cols, live, panels, VB, False).reshape(panel_rows, width)
        start = (row_index * panel_rows).astype(jnp.int32)
        current = lax.dynamic_slice_in_dim(total, start, panel_rows, 0)
        return lax.dynamic_update_slice_in_dim(total, current + part, start, 0)
    vertex_sums = lax.fori_loop(0, devices, vertex_device, jnp.zeros((NV, width), jnp.float32))
    out_y = (vertex_sums[:, :F] * vertex_scale[:, None]).astype(jnp.bfloat16)
    grad_z = (vertex_sums[:, F:] * vertex_scale[:, None]).astype(jnp.bfloat16)
    grad_x = jnp.dot(grad_z, theta.T, preferred_element_type=jnp.float32).astype(jnp.bfloat16)
    grad_theta = jnp.dot(features.T, grad_z, preferred_element_type=jnp.float32)
    return (out_y, grad_x, grad_theta, grad_w)
```

```python
import jax
import jax.numpy as jnp
from jax import lax
from jax.experimental import pallas as pl
from jax.experimental.pallas import tpu as pltpu
from jax.sharding import PartitionSpec as P

BF = jnp.bfloat16
F32 = jnp.float32
MESH = pl.DeviceIdType.MESH
T = 128
F = 256
VB = 32
EB = 24
SLOTS = 256
GF = (SLOTS + EB) // 2
GB = (SLOTS + VB) // 2
PARTS = 4
NSEM = 200


def plan(key, other, live, blocks, groups):
    t = jnp.arange(SLOTS, dtype=jnp.int32)
    alive = t < live
    key = jnp.where(alive, key, blocks)
    b = jnp.arange(blocks, dtype=jnp.int32)
    hit = key[:, None] == b[None, :]
    count = jnp.sum(hit.astype(jnp.int32), axis=0)
    padded = count + (count & 1)
    end = jnp.sum(jnp.where(b[None, :] <= b[:, None], padded[None, :], 0), axis=1)
    start = end - padded
    same = (key[:, None] == key[None, :]) & (t[None, :] < t[:, None])
    rank = jnp.sum(same.astype(jnp.int32), axis=1)
    place = jnp.sum(jnp.where(hit, start[None, :], 0), axis=1) + rank
    place = jnp.where(alive, place, -1)
    s = jnp.arange(2 * groups, dtype=jnp.int32)
    at = place[None, :] == s[:, None]
    tile = SLOTS + jnp.sum(jnp.where(at, t[None, :] - SLOTS, 0), axis=1)
    panel = jnp.sum(jnp.where(at, other[None, :], 0), axis=1)
    g2 = 2 * jnp.arange(groups, dtype=jnp.int32)
    keep = jnp.sum(
        ((start[None, :] < g2[:, None]) & (g2[:, None] < end[None, :])).astype(F32), axis=1
    )
    last = jnp.where(count > 0, end // 2, 0)
    return tile, panel, keep, last


def body(
    tile_f, panel_f, keep_f, last_f, tile_b, panel_b, keep_b, last_b,
    x_ref, g_ref, theta_ref, values_ref, vdeg_ref, ew_ref, ed_ref,
    y_ref, gx_ref, gt_ref, gw_ref,
    tiles, run, scale, theta_t,
    pt_z, pt_g, e_z, e_g,
    sib_s, sib_r, mine, zs, zr1, zr2, bxt, bzt, egt,
    vs, vr1, vr2, vkeep, ws, wr1, wr2, wkeep,
    gl, g1, gp1, g2, g3, go,
    tsem, ssem, rsem,
):
    i = lax.axis_index("vrow")
    j = lax.axis_index("ecol")
    z, core = i // 2, i % 2
    x, y = j // 4, j % 4

    def zc(d, c=None):
        return (((z + d) % 4) * 2 + (core if c is None else c), j)

    def xy(dx, dy):
        return (i, ((x + dx) % 4) * 4 + (y + dy) % 4)

    sib = (z * 2 + 1 - core, j)

    barrier = pltpu.get_barrier_semaphore()
    peers = [((i + d) % 8, j) for d in range(1, 8)]
    peers += [xy(d, 0) for d in (1, 2, 3)] + [xy(0, d) for d in (1, 2, 3)]
    for p in peers:
        pl.semaphore_signal(barrier, inc=1, device_id=p, device_id_type=MESH)

    load = pltpu.make_async_copy(values_ref, tiles.at[pl.ds(0, SLOTS)], tsem)
    load.start()

    deg = vdeg_ref[...].astype(F32)
    scale[...] = jnp.transpose(jnp.broadcast_to(1.0 / jnp.sqrt(deg), (F, 2 * T)))

    def prepare(src, dst):
        part = jnp.transpose(src[...].astype(F32) * scale[...]).astype(BF)
        for h in range(2):
            dst[2 * j + h] = part[:, h * T : (h + 1) * T]

    prepare(x_ref, pt_z)
    pl.semaphore_wait(barrier, len(peers))

    sent = []
    ids = [0]

    def send(src, dst, to):
        n = ids[0]
        ids[0] += 1
        copy = pltpu.make_async_remote_copy(
            src_ref=src, dst_ref=dst, send_sem=ssem.at[n], recv_sem=rsem.at[n],
            device_id=to, device_id_type=MESH,
        )
        copy.start()
        sent.append(copy)
        return copy

    def gather_row(pt):
        def block(h, a, b):
            dx, dy = (b, a) if h == 0 else (a, b)
            return pt.at[2 * (((x + dx) % 4) * 4 + (y + dy) % 4) + h]

        def to(h, a, b):
            return xy(b, a) if h == 0 else xy(a, b)

        def part(ref, up):
            return ref.at[pl.ds(0 if up else T, T)]

        def across(h, a):
            r = block(h, a, 0)
            return send(r, r, to(h, 0, 1)), send(r, r, to(h, 0, -1))

        def onward(h, a, b, up, where):
            r = part(block(h, a, b), up)
            return send(r, r, where)

        first, second, fwd = {}, {}, []
        for h in range(2):
            r = block(h, 0, 0)
            first[h] = send(r, r, to(h, 1, 0)), send(r, r, to(h, -1, 0))
        for h in range(2):
            second[h, 0] = across(h, 0)
        yield
        hop = {}
        for h in range(2):
            first[h][0].wait_recv()
            c = onward(h, -1, 0, True, to(h, 1, 0))
            first[h][1].wait_recv()
            hop[h] = c, onward(h, 1, 0, False, to(h, -1, 0))
        for h in range(2):
            second[h, -1] = across(h, -1)
            second[h, 1] = across(h, 1)
        yield

        def finish(a):
            for h in range(2):
                second[h, a][0].wait_recv()
                fwd.append(onward(h, a, -1, True, to(h, 0, 1)))
                second[h, a][1].wait_recv()
                fwd.append(onward(h, a, 1, False, to(h, 0, -1)))

        for h in range(2):
            for c in hop[h]:
                c.wait_recv()
            second[h, 2] = across(h, 2)
        finish(0)
        yield
        finish(-1)
        finish(1)
        yield
        finish(2)
        yield
        for c in fwd:
            c.wait_recv()

    def forward(pt, q):
        per = GF // PARTS
        unit = 5

        def turn(n, _):
            for u in range(unit):
                g = q * per + n * unit + u
                lhs = jnp.concatenate([pt[panel_f[2 * g]], pt[panel_f[2 * g + 1]]], axis=1)
                rhs = jnp.concatenate([tiles[tile_f[2 * g]], tiles[tile_f[2 * g + 1]]], axis=0)
                out = jnp.dot(lhs, rhs, preferred_element_type=F32)
                for h in range(2):
                    run[g + 1, h] = out[h * T : (h + 1) * T] + keep_f[g] * run[g, h]
            return 0

        lax.fori_loop(0, per // unit, turn, 0)

    def backward(e, q):
        per = GB // PARTS
        unit = 4

        def turn(n, _):
            for u in range(unit):
                g = q * per + n * unit + u
                lhs = jnp.concatenate([tiles[tile_b[2 * g]], tiles[tile_b[2 * g + 1]]], axis=1)
                rhs = jnp.concatenate([e[panel_b[2 * g]], e[panel_b[2 * g + 1]]], axis=0)
                out = jnp.dot(lhs, rhs, preferred_element_type=F32)
                for h in range(2):
                    run[g + 1, h] = out[:, h * T : (h + 1) * T] + keep_b[g] * run[g, h]
            return 0

        lax.fori_loop(0, per // unit, turn, 0)

    def reduce_col(k, finish):
        pair = {}
        for d in (2, 1, 3, 0):
            zd = (z + d) % 4
            for b in range(3):
                theirs = last_f[3 * (2 * zd + 1 - core) + b]
                ours = last_f[3 * (2 * zd + core) + b]
                for h in range(2):
                    rows = pl.ds(h * T, T)
                    sib_s[k, d, b, rows] = run[theirs, h].astype(BF)
                    mine[k, d, b, rows] = run[ours, h]
            pair[d] = send(sib_s.at[k, d], sib_r.at[k, d], sib)
        yield
        up, down = pl.ds(0, T), pl.ds(T, T)

        def join(d):
            pair[d].wait_recv()
            for b in range(3):
                mine[k, d, b] = mine[k, d, b] + sib_r[k, d, b].astype(F32)

        def pack(d, rows):
            for b in range(3):
                zs[k, d, b, rows] = mine[k, d, b, rows].astype(BF)

        join(2)
        pack(2, pl.ds(0, 2 * T))
        one = send(zs.at[k, 2, :, up], zr1.at[k, 0], zc(1))
        two = send(zs.at[k, 2, :, down], zr1.at[k, 1], zc(-1))
        join(1)
        pack(1, down)
        got = [send(zs.at[k, 1, :, down], zr2.at[k, 0, :, down], zc(1))]
        join(3)
        pack(3, up)
        got += [send(zs.at[k, 3, :, up], zr2.at[k, 1, :, up], zc(-1))]
        join(0)
        yield
        one.wait_recv()
        for b in range(3):
            zs[k, 1, b, up] = (mine[k, 1, b, up] + zr1[k, 0, b].astype(F32)).astype(BF)
        got += [send(zs.at[k, 1, :, up], zr2.at[k, 0, :, up], zc(1))]
        two.wait_recv()
        for b in range(3):
            zs[k, 3, b, down] = (mine[k, 3, b, down] + zr1[k, 1, b].astype(F32)).astype(BF)
        got += [send(zs.at[k, 3, :, down], zr2.at[k, 1, :, down], zc(-1))]
        yield
        for c in got:
            c.wait_recv()
        for b in range(3):
            total = mine[k, 0, b] + zr2[k, 0, b].astype(F32) + zr2[k, 1, b].astype(F32)
            finish(b, total)

    def split(value):
        hi = value.astype(BF)
        return hi, (value - hi.astype(F32)).astype(BF)

    def dot(a, b):
        return jnp.dot(a, b, preferred_element_type=F32)

    def coefs(b):
        cols = slice(b * T, (b + 1) * T)
        d = ed_ref[:, cols].astype(F32)
        return ew_ref[:, cols] / d, d

    def edges_z(b, total):
        hi, lo = split(total)
        bxt[b] = total
        bz = dot(theta_t[...], hi) + dot(theta_t[...], lo)
        bzt[b] = bz
        e_z[3 * i + b] = jnp.transpose(bz * coefs(b)[0]).astype(BF)

    def edges_g(b, total):
        coef, d = coefs(b)
        gw_ref[:, b * T : (b + 1) * T] = jnp.sum(bzt[b] * total, axis=0, keepdims=True) / d
        eg = total * coef
        egt[b] = eg
        hi, lo = split(eg)
        e_g[3 * i + b] = jnp.transpose(dot(theta_ref[...], hi) + dot(theta_ref[...], lo)).astype(BF)

    def gather_col(e):
        def shard(d, c=core):
            return e.at[pl.ds(3 * (2 * ((z + d) % 4) + c), 3)]

        def half(ref, up):
            return ref.at[:, pl.ds(0 if up else T // 2, T // 2)]

        def pass_on(ref, to):
            return send(ref, ref, to)

        right = pass_on(shard(0), zc(1))
        left = pass_on(shard(0), zc(-1))
        across = [pass_on(shard(0), sib)]
        yield
        right.wait_recv()
        far = [pass_on(half(shard(-1), True), zc(1))]
        left.wait_recv()
        far += [pass_on(half(shard(1), False), zc(-1))]
        across += [pass_on(shard(-1), sib), pass_on(shard(1), sib)]
        yield
        for c, up in zip(far, (True, False)):
            c.wait_recv()
            across += [pass_on(half(shard(2), up), sib)]
        yield
        for c in across:
            c.wait_recv()

    def reduce_row(k, out_ref):
        up, down = pl.ds(0, T // 2), pl.ds(T // 2, T // 2)

        def to(h, a, b):
            return xy(a, b) if h == 0 else xy(b, a)

        def fetch(h, p, q):
            dx, dy = (p, q) if h == 0 else (q, p)
            r = last_b[2 * (((x + dx) % 4) * 4 + (y + dy) % 4) + h]
            return jnp.concatenate([run[r, 0], run[r, 1]], axis=1)

        one, two, got = {}, {}, {}
        for h in range(2):
            for q in range(4):
                vs[k, h, 0, q] = fetch(h, 2, q).astype(BF)
            one[h] = send(vs.at[k, h, 0, :, up], vr1.at[k, h, 0], to(h, 1, 0))
            two[h] = send(vs.at[k, h, 0, :, down], vr1.at[k, h, 1], to(h, -1, 0))
        for h in range(2):
            for q in range(4):
                v = fetch(h, 1, q)
                vs[k, h, 1, q, down] = v[T // 2 :].astype(BF)
                vkeep[k, h, 1, q, up] = v[: T // 2]
                v = fetch(h, 3, q)
                vs[k, h, 2, q, up] = v[: T // 2].astype(BF)
                vkeep[k, h, 1, q, down] = v[T // 2 :]
            got[h] = [
                send(vs.at[k, h, 1, :, down], vr2.at[k, h, 0, :, down], to(h, 1, 0)),
                send(vs.at[k, h, 2, :, up], vr2.at[k, h, 1, :, up], to(h, -1, 0)),
            ]
        for h in range(2):
            for q in range(4):
                vkeep[k, h, 0, q] = fetch(h, 0, q)
        yield
        for h in range(2):
            one[h].wait_recv()
            for q in range(4):
                vs[k, h, 1, q, up] = (
                    vkeep[k, h, 1, q, up] + vr1[k, h, 0, q].astype(F32)
                ).astype(BF)
            got[h] += [send(vs.at[k, h, 1, :, up], vr2.at[k, h, 0, :, up], to(h, 1, 0))]
            two[h].wait_recv()
            for q in range(4):
                vs[k, h, 2, q, down] = (
                    vkeep[k, h, 1, q, down] + vr1[k, h, 1, q].astype(F32)
                ).astype(BF)
            got[h] += [send(vs.at[k, h, 2, :, down], vr2.at[k, h, 1, :, down], to(h, -1, 0))]
        yield
        one2, two2, got2 = {}, {}, {}
        for h in range(2):
            for c in got[h]:
                c.wait_recv()

            def total(q):
                return (
                    vkeep[k, h, 0, q]
                    + vr2[k, h, 0, q].astype(F32)
                    + vr2[k, h, 1, q].astype(F32)
                )

            ws[k, h, 0] = total(2).astype(BF)
            one2[h] = send(ws.at[k, h, 0, up], wr1.at[k, h, 0], to(h, 0, 1))
            two2[h] = send(ws.at[k, h, 0, down], wr1.at[k, h, 1], to(h, 0, -1))
            v = total(1)
            ws[k, h, 1, down] = v[T // 2 :].astype(BF)
            wkeep[k, h, 1, up] = v[: T // 2]
            v = total(3)
            ws[k, h, 2, up] = v[: T // 2].astype(BF)
            wkeep[k, h, 1, down] = v[T // 2 :]
            got2[h] = [
                send(ws.at[k, h, 1, down], wr2.at[k, h, 0, down], to(h, 0, 1)),
                send(ws.at[k, h, 2, up], wr2.at[k, h, 1, up], to(h, 0, -1)),
            ]
            wkeep[k, h, 0] = total(0)
        yield
        for h in range(2):
            one2[h].wait_recv()
            ws[k, h, 1, up] = (wkeep[k, h, 1, up] + wr1[k, h, 0].astype(F32)).astype(BF)
            got2[h] += [send(ws.at[k, h, 1, up], wr2.at[k, h, 0, up], to(h, 0, 1))]
            two2[h].wait_recv()
            ws[k, h, 2, down] = (wkeep[k, h, 1, down] + wr1[k, h, 1].astype(F32)).astype(BF)
            got2[h] += [send(ws.at[k, h, 2, down], wr2.at[k, h, 1, down], to(h, 0, -1))]
        yield
        for h in range(2):
            for c in got2[h]:
                c.wait_recv()
            v = wkeep[k, h, 0] + wr2[k, h, 0].astype(F32) + wr2[k, h, 1].astype(F32)
            rows = pl.ds(h * T, T)
            out_ref[rows] = (v * scale[rows]).astype(BF)

    def sum_theta():
        acc = jnp.zeros((F, F), F32)
        nt = (((1,), (1,)), ((), ()))
        for b in range(3):
            xh, xl = split(bxt[b])
            eh, el = split(egt[b])
            for a, c in ((xh, eh), (xl, eh), (xh, el)):
                acc = acc + lax.dot_general(a, c, nt, preferred_element_type=F32)
        gl[...] = acc
        got = []
        for d in range(1, 8):
            to = (i + d) % 8
            got.append(send(gl.at[pl.ds(32 * to, 32)], g1.at[d], (to, j)))
        yield
        own = gl[pl.ds(32 * i, 32)]
        for d, c in enumerate(got):
            c.wait_recv()
            own = own + g1[d + 1]
        gp1[...] = own
        got = []
        for d in (1, 2, 3):
            got.append(send(gp1.at[pl.ds(8 * ((x + d) % 4), 8)], g2.at[d], xy(d, 0)))
        yield
        own = gp1[pl.ds(8 * x, 8)]
        for d, c in enumerate(got):
            c.wait_recv()
            own = own + g2[d + 1]
        g3[y] = own
        got = [send(g3.at[y], g3.at[y], xy(0, d)) for d in (1, 2, 3)]
        yield
        for c in got:
            c.wait_recv()
        rows = pl.ds(32 * i + 8 * x, 8)
        go[rows] = ((g3[0] + g3[1]) + g3[2]) + g3[3]
        got = [send(go.at[rows], go.at[rows], xy(d, 0)) for d in (1, 2, 3)]
        yield
        for c in got:
            c.wait_recv()
        rows = pl.ds(32 * i, 32)
        got = [send(go.at[rows], go.at[rows], ((i + d) % 8, j)) for d in range(1, 8)]
        yield
        for c in got:
            c.wait_recv()
        gt_ref[...] = go[...]

    def step(gen):
        next(gen, None)

    def drain(gen):
        for _ in gen:
            pass

    row_z, row_g = gather_row(pt_z), gather_row(pt_g)
    step(row_z)
    prepare(g_ref, pt_g)
    theta_t[...] = jnp.transpose(theta_ref[...].astype(F32)).astype(BF)
    tiles[SLOTS] = jnp.zeros((T, T), BF)
    run[0] = jnp.zeros((2, T, T), F32)
    for _ in range(4):
        step(row_z)
    step(row_g)
    drain(row_z)
    load.wait()

    for q in range(PARTS):
        forward(pt_z, q)
        step(row_g)
    col_z, col_g = reduce_col(0, edges_z), reduce_col(1, edges_g)
    step(col_z)
    step(col_z)
    drain(row_g)
    forward(pt_g, 0)
    step(col_z)
    forward(pt_g, 1)
    drain(col_z)
    all_z, all_g = gather_col(e_z), gather_col(e_g)
    step(all_z)
    forward(pt_g, 2)
    step(all_z)
    forward(pt_g, 3)
    step(col_g)
    step(all_z)
    step(col_g)
    drain(all_z)
    backward(e_z, 0)
    step(col_g)
    backward(e_z, 1)
    drain(col_g)
    step(all_g)
    theta = sum_theta()
    step(theta)
    backward(e_z, 2)
    step(all_g)
    backward(e_z, 3)
    back_z, back_g = reduce_row(0, y_ref), reduce_row(1, gx_ref)
    step(back_z)
    step(all_g)
    step(theta)
    drain(all_g)
    backward(e_g, 0)
    step(back_z)
    step(theta)
    backward(e_g, 1)
    step(theta)
    step(back_z)
    backward(e_g, 2)
    step(theta)
    step(back_z)
    backward(e_g, 3)
    step(back_g)
    drain(back_z)
    drain(back_g)
    drain(theta)
    for c in sent:
        c.wait_send()


def shards(
    features, grad_out, theta, tile_values, tile_rows, tile_cols, tile_count,
    vertex_degree, edge_weight, edge_degree,
):
    live = tile_count[0]
    by_col = plan(tile_cols, tile_rows, live, EB, GF)
    by_row = plan(tile_rows, tile_cols, live, VB, GB)
    smem = pl.BlockSpec(memory_space=pltpu.SMEM)
    vmem = pl.BlockSpec(memory_space=pltpu.VMEM)
    hbm = pl.BlockSpec(memory_space=pl.ANY)
    v = pltpu.VMEM
    scratch = [
        v((SLOTS + 1, T, T), BF),
        v((GB + 1, 2, T, T), F32),
        v((2 * T, F), F32),
        v((F, F), BF),
        v((VB, F, T), BF),
        v((VB, F, T), BF),
        v((EB, T, F), BF),
        v((EB, T, F), BF),
        v((2, 4, 3, F, T), BF),
        v((2, 4, 3, F, T), BF),
        v((2, 4, 3, F, T), F32),
        v((2, 4, 3, F, T), BF),
        v((2, 2, 3, T, T), BF),
        v((2, 2, 3, F, T), BF),
        v((3, F, T), F32),
        v((3, F, T), F32),
        v((3, F, T), F32),
        v((2, 2, 3, 4, T, F), BF),
        v((2, 2, 2, 4, T // 2, F), BF),
        v((2, 2, 2, 4, T, F), BF),
        v((2, 2, 2, 4, T, F), F32),
        v((2, 2, 3, T, F), BF),
        v((2, 2, 2, T // 2, F), BF),
        v((2, 2, 2, T, F), BF),
        v((2, 2, 2, T, F), F32),
        v((F, F), F32),
        v((8, 32, F), F32),
        v((32, F), F32),
        v((4, 8, F), F32),
        v((4, 8, F), F32),
        v((F, F), F32),
        pltpu.SemaphoreType.DMA,
        pltpu.SemaphoreType.DMA((NSEM,)),
        pltpu.SemaphoreType.DMA((NSEM,)),
    ]
    return pl.pallas_call(
        body,
        out_shape=(
            jax.ShapeDtypeStruct((2 * T, F), BF),
            jax.ShapeDtypeStruct((2 * T, F), BF),
            jax.ShapeDtypeStruct((F, F), F32),
            jax.ShapeDtypeStruct((1, 3 * T), F32),
        ),
        in_specs=[smem] * 8 + [vmem] * 3 + [hbm] + [vmem] * 3,
        out_specs=[vmem] * 4,
        scratch_shapes=scratch,
        compiler_params=pltpu.CompilerParams(
            collective_id=0, has_side_effects=True, vmem_limit_bytes=62 * 1024 * 1024
        ),
        cost_estimate=pl.CostEstimate(
            flops=20_000_000_000, bytes_accessed=10_000_000, transcendentals=0
        ),
    )(
        *by_col, *by_row, features, grad_out, theta, tile_values,
        vertex_degree.reshape(1, 2 * T), edge_weight, edge_degree,
    )


def solution(mesh):
    both = ("vrow", "ecol")
    in_specs = (
        P(both, None), P(both, None), P(), P(both, None, None), P(both), P(both), P(both),
        P(both), P("ecol", "vrow"), P("ecol", "vrow"),
    )
    out_specs = (P(both, None), P(both, None), P(), P("ecol", "vrow"))
    return jax.shard_map(shards, mesh=mesh, in_specs=in_specs, out_specs=out_specs, check_vma=False)
```

```python
import jax
import jax.numpy as jnp
from jax import lax
from jax.experimental import pallas as pl
from jax.experimental.pallas import tpu as pltpu
from jax.sharding import PartitionSpec as P

BF = jnp.bfloat16
F32 = jnp.float32
MESH = pl.DeviceIdType.MESH
T = 128
F = 256
VB = 32
EB = 24
SLOTS = 256
GF = (SLOTS + EB) // 2
GB = (SLOTS + VB) // 2
PARTS = 2
NSEND = 29
NRECV = 57


def plan(key, other, live, pad):
    n = SLOTS

    def iota(shape, dim):
        return lax.broadcasted_iota(jnp.int32, shape, dim).astype(F32)

    key_l = jnp.broadcast_to(key.astype(F32), (n, n))
    key_l = jnp.where(iota((n, n), 1) < live, key_l, float(n))
    key_s = jnp.transpose(key_l)
    other_s = jnp.transpose(jnp.broadcast_to(other.astype(F32), (n, n)))
    t = iota((n, n), 0)
    same = jnp.where((key_s == key_l) & (iota((n, n), 1) < t), 1.0, 0.0)
    rank = jnp.sum(same, axis=1, keepdims=True)
    hit = jnp.where(key_s[:, :T] == iota((n, T), 1), 1.0, 0.0)
    count = jnp.sum(hit, axis=0, keepdims=True)
    half = jnp.floor((count + 1.0) * 0.5)
    upto = jnp.where(iota((T, T), 0) <= iota((T, T), 1), 1.0, 0.0)
    end = jnp.dot(
        jnp.broadcast_to(half, (8, T)).astype(BF), upto.astype(BF), preferred_element_type=F32
    )[:1]
    start = 2.0 * (end - half)
    place = jnp.sum(hit * start, axis=1, keepdims=True) + rank
    place = jnp.where(key_s[:, :1] < float(n), place, -1.0)
    at = jnp.where(place == iota((n, pad), 1), 1.0, 0.0)
    tile = jnp.sum(at * (t[:, :1] - float(n)), axis=0, keepdims=True) + float(n)
    panel = jnp.sum(at * other_s[:, :1], axis=0, keepdims=True)
    more = jnp.where(rank > 0.0, 1.0, 0.0)
    keep = jnp.sum(jnp.where(place == 2.0 * iota((n, pad), 1), more, 0.0), axis=0, keepdims=True)
    last = jnp.where(count > 0.0, end, 0.0)
    last = jnp.concatenate([last, jnp.zeros((1, pad - T), F32)], axis=1)
    rows = jnp.concatenate([tile, panel, keep, last, jnp.zeros((4, pad), F32)], axis=0)
    return rows.astype(jnp.int32)


def order_tiles(count_ref, rows_ref, cols_ref, by_col, by_row):
    live = count_ref[0].astype(F32)
    by_col[...] = plan(cols_ref[...], rows_ref[...], live, 384)
    by_row[...] = plan(rows_ref[...], cols_ref[...], live, 384)


def body(
    by_col, by_row,
    x_ref, g_ref, theta_ref, values_ref, vdeg_ref, ew_ref, ed_ref,
    y_ref, gz_ref, gt_ref, gw_ref,
    tiles, run, scale, theta_t,
    pt_0, pt_1, pt_2, pt_3, e_0, e_1, e_2, e_3,
    sib_s, sib_r, mine, zs, zr, bxt, bgt, vs, vr, vkeep, ws, wr,
    gl, g1, gp1, g2, g3, go,
    tsem, ssem, rsem,
):
    pts, es = (pt_0, pt_1, pt_2, pt_3), (e_0, e_1, e_2, e_3)
    i = lax.axis_index("vrow")
    j = lax.axis_index("ecol")
    z, core = i // 2, i % 2
    x, y = j // 4, j % 4

    def zc(d, c=None):
        return (((z + d) % 4) * 2 + (core if c is None else c), j)

    def xy(dx, dy):
        return (i, ((x + dx) % 4) * 4 + (y + dy) % 4)

    sib = (z * 2 + 1 - core, j)

    barrier = pltpu.get_barrier_semaphore()
    peers = [((i + d) % 8, j) for d in range(1, 8)]
    peers += [xy(d, 0) for d in (1, 2, 3)] + [xy(0, d) for d in (1, 2, 3)]
    for p in peers:
        pl.semaphore_signal(barrier, inc=1, device_id=p, device_id_type=MESH)

    load = pltpu.make_async_copy(values_ref, tiles.at[pl.ds(0, SLOTS)], tsem)
    load.start()

    deg = vdeg_ref[...].astype(F32)
    scale[...] = jnp.transpose(jnp.broadcast_to(1.0 / jnp.sqrt(deg), (F, 2 * T)))

    def prepare(src, k):
        part = jnp.transpose(src[...].astype(F32) * scale[...]).astype(BF)
        for c in range(2):
            for h in range(2):
                pts[k + c][2 * j + h] = part[c * T : (c + 1) * T, h * T : (h + 1) * T]

    prepare(x_ref, 0)
    pl.semaphore_wait(barrier, len(peers))

    sends, groups = [], [0, 0]

    def send(src, dst, to, out, into):
        pltpu.make_async_remote_copy(
            src_ref=src, dst_ref=dst, send_sem=ssem.at[out], recv_sem=rsem.at[into],
            device_id=to, device_id_type=MESH,
        ).start()

    def leaving(ref):
        n = groups[0]
        groups[0] += 1
        sends.append((ref, n))
        return n

    def coming():
        groups[1] += 1
        return groups[1] - 1

    def arrived(ref, n):
        pltpu.make_async_copy(ref, ref, rsem.at[n]).wait()

    near = (1, 3, 2)

    def gather_row(k):
        pt = pts[k]

        def to(h, a, b):
            return xy(b, a) if h == 0 else xy(a, b)

        out, one, two = leaving(pt.at[pl.ds(0, 30)]), coming(), coming()
        own = [pt.at[2 * j + h] for h in range(2)]
        for d in near:
            for h in range(2):
                send(own[h], own[h], to(h, d, 0), out, one)
        for d in near:
            for h in range(2):
                send(own[h], own[h], to(h, 0, d), out, two)
        yield
        arrived(pt.at[pl.ds(0, 6)], one)
        for a in near:
            for d in near:
                for h in range(2):
                    dx, dy = (0, a) if h == 0 else (a, 0)
                    r = pt.at[2 * (((x + dx) % 4) * 4 + (y + dy) % 4) + h]
                    send(r, r, to(h, 0, d), out, two)
        yield
        arrived(pt.at[pl.ds(0, 24)], two)

    def sweep(table, groups, unit, part, product):
        per = groups // PARTS

        def turn(n, acc):
            for u in range(unit):
                g = part * per + n * unit + u
                acc = product(2 * g) + table[2, g].astype(F32) * acc
                run[g + 1] = acc
            return acc

        lax.fori_loop(0, per // unit, turn, run[part * per])

    def dot(a, b):
        return jnp.dot(a, b, preferred_element_type=F32)

    def forward(k, part):
        pt = pts[k]

        def product(s):
            lhs = jnp.concatenate([pt[by_col[1, s]], pt[by_col[1, s + 1]]], axis=1)
            rhs = jnp.concatenate([tiles[by_col[0, s]], tiles[by_col[0, s + 1]]], axis=0)
            return dot(lhs, rhs)

        sweep(by_col, GF, 35, part, product)

    def backward(k, part):
        e = es[k]

        def product(s):
            lhs = jnp.concatenate([tiles[by_row[0, s]], tiles[by_row[0, s + 1]]], axis=1)
            rhs = jnp.concatenate([e[by_row[1, s]], e[by_row[1, s + 1]]], axis=0)
            return dot(lhs, rhs)

        sweep(by_row, GB, 36, part, product)

    def split(value):
        hi = value.astype(BF)
        return hi, (value - hi.astype(F32)).astype(BF)

    def coefs(b):
        cols = slice(b * T, (b + 1) * T)
        d = ed_ref[:, cols].astype(F32)
        return ew_ref[:, cols] / d, d

    def reduce_col(k):
        order = (2, 1, 3, 0)
        out, out2 = leaving(sib_s.at[k]), leaving(zs.at[k])
        pair, into = [coming() for _ in range(4)], coming()
        for d in order:
            zd = (z + d) % 4
            for b in range(3):
                sib_s[k, d, b] = run[by_col[3, 3 * (2 * zd + 1 - core) + b]].astype(BF)
            send(sib_s.at[k, d], sib_r.at[k, d], sib, out, pair[d])
        for d in order:
            zd = (z + d) % 4
            for b in range(3):
                mine[k, d, b] = run[by_col[3, 3 * (2 * zd + core) + b]]
        yield
        for d in order:
            arrived(sib_r.at[k, d], pair[d])
            for b in range(3):
                total = mine[k, d, b] + sib_r[k, d, b].astype(F32)
                if d == 0:
                    mine[k, 0, b] = total
                else:
                    zs[k, d - 1, b] = total.astype(BF)
            if d:
                send(zs.at[k, d - 1], zr.at[k, d - 1], zc(d), out2, into)
        yield
        arrived(zr.at[k], into)
        for b in range(3):
            total = mine[k, 0, b]
            for d in (1, 2, 3):
                total = total + zr[k, d - 1, b].astype(F32)
            if k < 2:
                bxt[k, b] = total
            else:
                bgt[k - 2, b] = total
            es[k][3 * i + b] = jnp.transpose(total * coefs(b)[0]).astype(BF)

    def gather_col(k):
        def shard(d):
            return es[k].at[pl.ds(3 * (2 * ((z + d) % 4) + core), 3)]

        out, across = leaving(es[k].at[pl.ds(0, 21)]), coming()
        own = {d: coming() for d in (2, 1, 3)}
        for d in own:
            send(shard(0), shard(0), zc(d), out, own[d])
        send(shard(0), shard(0), sib, out, across)

        def pass_on(d):
            arrived(shard(-d), own[d])
            send(shard(-d), shard(-d), sib, out, across)

        yield
        pass_on(1)
        pass_on(3)
        yield
        pass_on(2)
        yield
        arrived(es[k].at[pl.ds(0, 12)], across)

    def weights_grad():
        for b in range(3):
            hi, lo = zip(*[split(bxt[c, b]) for c in range(2)])
            hi, lo = jnp.concatenate(hi, axis=0), jnp.concatenate(lo, axis=0)
            bz = dot(theta_t[...], hi) + dot(theta_t[...], lo)
            terms = bz[:T] * bgt[0, b] + bz[T:] * bgt[1, b]
            cols = slice(b * T, (b + 1) * T)
            gw_ref[:, cols] = jnp.sum(terms, axis=0, keepdims=True) / coefs(b)[1]

    def reduce_row(k):
        def to(h, a, b):
            return xy(a, b) if h == 0 else xy(b, a)

        def fetch(h, p, q):
            dx, dy = (p, q) if h == 0 else (q, p)
            return run[by_row[3, 2 * (((x + dx) % 4) * 4 + (y + dy) % 4) + h]]

        out, out2, one, two = leaving(vs.at[k]), leaving(ws.at[k]), coming(), coming()
        for p in near:
            for h in range(2):
                for q in range(4):
                    vs[k, h, p - 1, q] = fetch(h, p, q).astype(BF)
                send(vs.at[k, h, p - 1], vr.at[k, h, p - 1], to(h, p, 0), out, one)
        for h in range(2):
            for q in range(4):
                vkeep[k, h, q] = fetch(h, 0, q)
        yield
        arrived(vr.at[k], one)
        for q in (1, 3, 2, 0):
            for h in range(2):
                total = vkeep[k, h, q]
                for p in range(3):
                    total = total + vr[k, h, p, q].astype(F32)
                if q:
                    ws[k, h, q - 1] = total.astype(BF)
                    send(ws.at[k, h, q - 1], wr.at[k, h, q - 1], to(h, 0, q), out2, two)
                else:
                    vkeep[k, h, 0] = total
        yield
        arrived(wr.at[k], two)
        for h in range(2):
            v = vkeep[k, h, 0]
            for q in range(3):
                v = v + wr[k, h, q].astype(F32)
            rows = pl.ds(h * T, T)
            cols = pl.ds((k % 2) * T, T)
            v = v * scale[rows, :T]
            if k < 2:
                y_ref[rows, cols] = v
            else:
                gz_ref[rows, cols] = v.astype(BF)

    def sum_theta():
        nt = (((1,), (1,)), ((), ()))
        for w in range(2):
            acc = jnp.zeros((F, T), F32)
            for b in range(3):
                xs = [split(bxt[c, b]) for c in range(2)]
                xh, xl = [jnp.concatenate([p[m] for p in xs], axis=0) for m in range(2)]
                eh, el = split(bgt[w, b] * coefs(b)[0])
                for p, q in ((xh, eh), (xl, eh), (xh, el)):
                    acc = acc + lax.dot_general(p, q, nt, preferred_element_type=F32)
            gl[:, w * T : (w + 1) * T] = acc
        out = [leaving(gl.at[pl.ds(0, 224)]), leaving(gp1.at[pl.ds(0, 24)]), leaving(g3.at[pl.ds(0, 3)])]
        out += [leaving(go.at[pl.ds(0, 24)]), leaving(go.at[pl.ds(0, 224)])]
        into = [coming() for _ in range(5)]
        for d in range(1, 8):
            to = (i + d) % 8
            send(gl.at[pl.ds(32 * to, 32)], g1.at[d - 1], (to, j), out[0], into[0])
        yield
        arrived(g1, into[0])
        own = gl[pl.ds(32 * i, 32)]
        for d in range(7):
            own = own + g1[d]
        gp1[...] = own
        for d in near:
            send(gp1.at[pl.ds(8 * ((x + d) % 4), 8)], g2.at[d - 1], xy(d, 0), out[1], into[1])
        yield
        arrived(g2, into[1])
        g3[y] = gp1[pl.ds(8 * x, 8)] + g2[0] + g2[1] + g2[2]
        for d in near:
            send(g3.at[y], g3.at[y], xy(0, d), out[2], into[2])
        yield
        arrived(g3.at[pl.ds(0, 3)], into[2])
        rows = pl.ds(32 * i + 8 * x, 8)
        go[rows] = ((g3[0] + g3[1]) + g3[2]) + g3[3]
        for d in near:
            send(go.at[rows], go.at[rows], xy(d, 0), out[3], into[3])
        yield
        arrived(go.at[pl.ds(0, 24)], into[3])
        rows = pl.ds(32 * i, 32)
        for d in range(1, 8):
            send(go.at[rows], go.at[rows], ((i + d) % 8, j), out[4], into[4])
        yield
        arrived(go.at[pl.ds(0, 224)], into[4])
        gt_ref[...] = go[...]

    def step(gen):
        next(gen, None)

    def drain(gen):
        for _ in gen:
            pass

    row = [gather_row(k) for k in range(4)]
    col = [reduce_col(k) for k in range(4)]
    full = [gather_col(k) for k in range(4)]
    back = [reduce_row(k) for k in range(4)]
    theta = sum_theta()
    def tables():
        theta_t[...] = jnp.transpose(theta_ref[...].astype(F32)).astype(BF)
        tiles[SLOTS] = jnp.zeros((T, T), BF)
        run[0] = jnp.zeros((T, T), F32)

    step(row[0])
    step(row[1])
    prepare(g_ref, 2)
    step(row[2])
    tables()
    step(row[3])
    step(row[0])
    step(row[1])
    step(row[2])
    step(row[3])
    step(row[0])
    load.wait()
    forward(0, 0)
    forward(0, 1)
    step(col[0])
    step(row[1])
    forward(1, 0)
    step(col[0])
    forward(1, 1)
    step(col[1])
    step(row[2])
    forward(2, 0)
    step(col[1])
    forward(2, 1)
    step(col[2])
    step(row[3])
    forward(3, 0)
    step(col[0])
    step(full[0])
    step(col[2])
    forward(3, 1)
    step(col[3])
    step(col[1])
    step(full[1])
    step(col[3])
    step(full[0])
    step(full[0])
    step(full[0])
    backward(0, 0)
    backward(0, 1)
    step(back[0])
    step(col[2])
    step(full[2])
    step(full[1])
    step(full[1])
    step(full[1])
    backward(1, 0)
    backward(1, 1)
    step(col[3])
    step(theta)
    step(back[0])
    step(back[1])
    weights_grad()
    step(full[3])
    step(full[2])
    step(full[2])
    step(full[2])
    backward(2, 0)
    step(back[0])
    backward(2, 1)
    step(theta)
    step(back[2])
    step(full[3])
    step(full[3])
    step(theta)
    step(back[1])
    step(full[3])
    backward(3, 0)
    backward(3, 1)
    step(back[3])
    step(theta)
    step(back[2])
    step(back[1])
    step(theta)
    step(back[3])
    step(back[2])
    step(back[3])
    step(theta)
    for ref, n in sends:
        pltpu.make_async_copy(ref, ref, ssem.at[n]).wait()


def tail(ys_ref, gz_ref, gt_ref, gw_ref, theta_ref, y_out, gx_out, gt_out, gw_out):
    theta = theta_ref[...]
    ys = ys_ref[...]
    hi = ys.astype(BF)
    lo = (ys - hi.astype(F32)).astype(BF)
    y = jnp.dot(hi, theta, preferred_element_type=F32)
    y_out[...] = (y + jnp.dot(lo, theta, preferred_element_type=F32)).astype(BF)
    nt = (((1,), (1,)), ((), ()))
    gx_out[...] = lax.dot_general(gz_ref[...], theta, nt, preferred_element_type=F32).astype(BF)
    gt_out[...] = gt_ref[...]
    gw_out[...] = gw_ref[...]


def shards(
    features, grad_out, theta, tile_values, tile_rows, tile_cols, tile_count,
    vertex_degree, edge_weight, edge_degree,
):
    smem = pl.BlockSpec(memory_space=pltpu.SMEM)
    vmem = pl.BlockSpec(memory_space=pltpu.VMEM)
    hbm = pl.BlockSpec(memory_space=pl.ANY)
    v = pltpu.VMEM
    scratch = [
        v((SLOTS + 1, T, T), BF),
        v((GB + 1, T, T), F32),
        v((2 * T, F), F32),
        v((F, F), BF),
        *[v((VB, T, T), BF)] * 4,
        *[v((EB, T, T), BF)] * 4,
        v((4, 4, 3, T, T), BF),
        v((4, 4, 3, T, T), BF),
        v((4, 4, 3, T, T), F32),
        v((4, 3, 3, T, T), BF),
        v((4, 3, 3, T, T), BF),
        v((2, 3, T, T), F32),
        v((2, 3, T, T), F32),
        v((4, 2, 3, 4, T, T), BF),
        v((4, 2, 3, 4, T, T), BF),
        v((4, 2, 4, T, T), F32),
        v((4, 2, 3, T, T), BF),
        v((4, 2, 3, T, T), BF),
        v((F, F), F32),
        v((7, 32, F), F32),
        v((32, F), F32),
        v((3, 8, F), F32),
        v((4, 8, F), F32),
        v((F, F), F32),
        pltpu.SemaphoreType.DMA,
        pltpu.SemaphoreType.DMA((NSEND,)),
        pltpu.SemaphoreType.DMA((NRECV,)),
    ]
    table = jax.ShapeDtypeStruct((8, 384), jnp.int32)
    by_col, by_row = pl.pallas_call(
        order_tiles,
        out_shape=(table, table),
        in_specs=[smem, vmem, vmem],
        out_specs=[vmem] * 2,
        cost_estimate=pl.CostEstimate(flops=1_000_000, bytes_accessed=30_000, transcendentals=0),
    )(tile_count, tile_rows.reshape(1, SLOTS), tile_cols.reshape(1, SLOTS))
    ys, gz, gt, gw = pl.pallas_call(
        body,
        out_shape=(
            jax.ShapeDtypeStruct((2 * T, F), F32),
            jax.ShapeDtypeStruct((2 * T, F), BF),
            jax.ShapeDtypeStruct((F, F), F32),
            jax.ShapeDtypeStruct((1, 3 * T), F32),
        ),
        in_specs=[smem] * 2 + [vmem] * 3 + [hbm] + [vmem] * 3,
        out_specs=[vmem] * 4,
        scratch_shapes=scratch,
        compiler_params=pltpu.CompilerParams(
            collective_id=0, has_side_effects=True, vmem_limit_bytes=60 * 1024 * 1024
        ),
        cost_estimate=pl.CostEstimate(
            flops=20_000_000_000, bytes_accessed=10_000_000, transcendentals=0
        ),
    )(
        by_col, by_row, features, grad_out, theta, tile_values, vertex_degree.reshape(1, 2 * T),
        edge_weight, edge_degree,
    )
    return pl.pallas_call(
        tail,
        out_shape=(
            jax.ShapeDtypeStruct((2 * T, F), BF),
            jax.ShapeDtypeStruct((2 * T, F), BF),
            jax.ShapeDtypeStruct((F, F), F32),
            jax.ShapeDtypeStruct((1, 3 * T), F32),
        ),
        in_specs=[vmem] * 5,
        out_specs=[vmem] * 4,
        cost_estimate=pl.CostEstimate(flops=100_000_000, bytes_accessed=2_000_000, transcendentals=0),
    )(ys, gz, gt, gw, theta)


def solution(mesh):
    both = ("vrow", "ecol")
    in_specs = (
        P(both, None), P(both, None), P(), P(both, None, None), P(both), P(both), P(both),
        P(both), P("ecol", "vrow"), P("ecol", "vrow"),
    )
    out_specs = (P(both, None), P(both, None), P(), P("ecol", "vrow"))
    return jax.shard_map(shards, mesh=mesh, in_specs=in_specs, out_specs=out_specs, check_vma=False)
```

```python
import jax
import jax.numpy as jnp
from jax import lax
from jax.experimental import pallas as pl
from jax.experimental.pallas import tpu as pltpu
from jax.sharding import PartitionSpec as P

BF = jnp.bfloat16
F32 = jnp.float32
MESH = pl.DeviceIdType.MESH
T = 128
F = 256
VB = 32
EB = 24
SLOTS = 256
GF = (SLOTS + EB) // 2
GB = (SLOTS + VB) // 2
PARTS = 2
NSEND = 29
NRECV = 69


def plan(key, other, live, pad):
    n = SLOTS

    def iota(shape, dim):
        return lax.broadcasted_iota(jnp.int32, shape, dim).astype(F32)

    key_l = jnp.broadcast_to(key.astype(F32), (n, n))
    key_l = jnp.where(iota((n, n), 1) < live, key_l, float(n))
    key_s = jnp.transpose(key_l)
    other_s = jnp.transpose(jnp.broadcast_to(other.astype(F32), (n, n)))
    t = iota((n, n), 0)
    same = jnp.where((key_s == key_l) & (iota((n, n), 1) < t), 1.0, 0.0)
    rank = jnp.sum(same, axis=1, keepdims=True)
    hit = jnp.where(key_s[:, :T] == iota((n, T), 1), 1.0, 0.0)
    count = jnp.sum(hit, axis=0, keepdims=True)
    half = jnp.floor((count + 1.0) * 0.5)
    upto = jnp.where(iota((T, T), 0) <= iota((T, T), 1), 1.0, 0.0)
    end = jnp.dot(
        jnp.broadcast_to(half, (8, T)).astype(BF), upto.astype(BF), preferred_element_type=F32
    )[:1]
    start = 2.0 * (end - half)
    place = jnp.sum(hit * start, axis=1, keepdims=True) + rank
    place = jnp.where(key_s[:, :1] < float(n), place, -1.0)
    at = jnp.where(place == iota((n, pad), 1), 1.0, 0.0)
    tile = jnp.sum(at * (t[:, :1] - float(n)), axis=0, keepdims=True) + float(n)
    panel = jnp.sum(at * other_s[:, :1], axis=0, keepdims=True)
    more = jnp.where(rank > 0.0, 1.0, 0.0)
    keep = jnp.sum(jnp.where(place == 2.0 * iota((n, pad), 1), more, 0.0), axis=0, keepdims=True)
    last = jnp.where(count > 0.0, end, 0.0)
    last = jnp.concatenate([last, jnp.zeros((1, pad - T), F32)], axis=1)
    rows = jnp.concatenate([tile, panel, keep, last, jnp.zeros((4, pad), F32)], axis=0)
    return rows.astype(jnp.int32)


def order_tiles(count_ref, rows_ref, cols_ref, by_col, by_row):
    live = count_ref[0].astype(F32)
    by_col[...] = plan(cols_ref[...], rows_ref[...], live, 384)
    by_row[...] = plan(rows_ref[...], cols_ref[...], live, 384)


def body(
    by_col, by_row,
    x_ref, g_ref, theta_ref, values_ref, vdeg_ref, ew_ref, ed_ref,
    y_ref, gz_ref, gt_ref, gw_ref,
    tiles, run, scale, theta_t,
    pt_0, pt_1, pt_2, pt_3, e_0, e_1, e_2, e_3,
    sib_s, sib_r, mine, zs, zr, bxt, bgt, vs, vr1, vr2, vkeep, ws, wr,
    gl, g1, gp1, g2, g3, go,
    tsem, ssem, rsem,
):
    pts, es = (pt_0, pt_1, pt_2, pt_3), (e_0, e_1, e_2, e_3)
    i = lax.axis_index("vrow")
    j = lax.axis_index("ecol")
    z, core = i // 2, i % 2
    x, y = j // 4, j % 4

    def zc(d, c=None):
        return (((z + d) % 4) * 2 + (core if c is None else c), j)

    def xy(dx, dy):
        return (i, ((x + dx) % 4) * 4 + (y + dy) % 4)

    sib = (z * 2 + 1 - core, j)

    barrier = pltpu.get_barrier_semaphore()
    peers = [((i + d) % 8, j) for d in range(1, 8)]
    peers += [xy(d, 0) for d in (1, 2, 3)] + [xy(0, d) for d in (1, 2, 3)]
    for p in peers:
        pl.semaphore_signal(barrier, inc=1, device_id=p, device_id_type=MESH)

    load = pltpu.make_async_copy(values_ref, tiles.at[pl.ds(0, SLOTS)], tsem)
    load.start()

    deg = vdeg_ref[...].astype(F32)
    scale[...] = jnp.transpose(jnp.broadcast_to(1.0 / jnp.sqrt(deg), (F, 2 * T)))

    def prepare(src, k):
        part = jnp.transpose(src[...].astype(F32) * scale[...]).astype(BF)
        for c in range(2):
            for h in range(2):
                pts[k + c][2 * j + h] = part[c * T : (c + 1) * T, h * T : (h + 1) * T]

    prepare(x_ref, 0)
    pl.semaphore_wait(barrier, len(peers))

    sends, groups = [], [0, 0]

    def send(src, dst, to, out, into):
        pltpu.make_async_remote_copy(
            src_ref=src, dst_ref=dst, send_sem=ssem.at[out], recv_sem=rsem.at[into],
            device_id=to, device_id_type=MESH,
        ).start()

    def leaving(ref):
        n = groups[0]
        groups[0] += 1
        sends.append((ref, n))
        return n

    def coming():
        groups[1] += 1
        return groups[1] - 1

    def arrived(ref, n):
        pltpu.make_async_copy(ref, ref, rsem.at[n]).wait()

    near = (1, 3, 2)

    def gather_row(k):
        pt = pts[k]

        def to(h, a, b):
            return xy(b, a) if h == 0 else xy(a, b)

        def block(h, a, b):
            dx, dy = (b, a) if h == 0 else (a, b)
            return pt.at[2 * (((x + dx) % 4) * 4 + (y + dy) % 4) + h]

        out = leaving(pt.at[pl.ds(0, 30)])
        one, two, three, four = [coming() for _ in range(4)]
        for d in near:
            for h in range(2):
                send(block(h, 0, 0), block(h, 0, 0), to(h, d, 0), out, one)

        def across(a, into):
            for d in (1, -1):
                for h in range(2):
                    send(block(h, a, 0), block(h, a, 0), to(h, 0, d), out, into)

        def onward(a):
            for d, start in ((1, 0), (-1, T // 2)):
                for h in range(2):
                    r = block(h, a, -d).at[pl.ds(start, T // 2)]
                    send(r, r, to(h, 0, d), out, four)

        across(0, two)
        yield
        arrived(pt.at[pl.ds(0, 6)], one)
        for a in near:
            across(a, three)
        yield
        arrived(pt.at[pl.ds(0, 4)], two)
        onward(0)
        yield
        arrived(pt.at[pl.ds(0, 12)], three)
        for a in near:
            onward(a)
        yield
        arrived(pt.at[pl.ds(0, 8)], four)

    def sweep(table, groups, unit, part, product):
        per = groups // PARTS

        def turn(n, acc):
            for u in range(unit):
                g = part * per + n * unit + u
                acc = product(2 * g) + table[2, g].astype(F32) * acc
                run[g + 1] = acc
            return acc

        lax.fori_loop(0, per // unit, turn, run[part * per])

    def dot(a, b):
        return jnp.dot(a, b, preferred_element_type=F32)

    def forward(k, part):
        pt = pts[k]

        def product(s):
            lhs = jnp.concatenate([pt[by_col[1, s]], pt[by_col[1, s + 1]]], axis=1)
            rhs = jnp.concatenate([tiles[by_col[0, s]], tiles[by_col[0, s + 1]]], axis=0)
            return dot(lhs, rhs)

        sweep(by_col, GF, 35, part, product)

    def backward(k, part):
        e = es[k]

        def product(s):
            lhs = jnp.concatenate([tiles[by_row[0, s]], tiles[by_row[0, s + 1]]], axis=1)
            rhs = jnp.concatenate([e[by_row[1, s]], e[by_row[1, s + 1]]], axis=0)
            return dot(lhs, rhs)

        sweep(by_row, GB, 36, part, product)

    def split(value):
        hi = value.astype(BF)
        return hi, (value - hi.astype(F32)).astype(BF)

    def coefs(b):
        cols = slice(b * T, (b + 1) * T)
        d = ed_ref[:, cols].astype(F32)
        return ew_ref[:, cols] / d, d

    def reduce_col(k):
        order = (2, 1, 3, 0)
        out, out2 = leaving(sib_s.at[k]), leaving(zs.at[k])
        pair, into = [coming() for _ in range(4)], coming()
        for d in order:
            zd = (z + d) % 4
            for b in range(3):
                sib_s[k, d, b] = run[by_col[3, 3 * (2 * zd + 1 - core) + b]].astype(BF)
            send(sib_s.at[k, d], sib_r.at[k, d], sib, out, pair[d])
        for d in order:
            zd = (z + d) % 4
            for b in range(3):
                mine[k, d, b] = run[by_col[3, 3 * (2 * zd + core) + b]]
        yield
        for d in order:
            arrived(sib_r.at[k, d], pair[d])
            for b in range(3):
                total = mine[k, d, b] + sib_r[k, d, b].astype(F32)
                if d == 0:
                    mine[k, 0, b] = total
                else:
                    zs[k, d - 1, b] = total.astype(BF)
            if d:
                send(zs.at[k, d - 1], zr.at[k, d - 1], zc(d), out2, into)
        yield
        arrived(zr.at[k], into)
        for b in range(3):
            total = mine[k, 0, b]
            for d in (1, 2, 3):
                total = total + zr[k, d - 1, b].astype(F32)
            if k < 2:
                bxt[k, b] = total
            else:
                bgt[k - 2, b] = total
            es[k][3 * i + b] = jnp.transpose(total * coefs(b)[0]).astype(BF)

    def gather_col(k):
        def shard(d):
            return es[k].at[pl.ds(3 * (2 * ((z + d) % 4) + core), 3)]

        out, across = leaving(es[k].at[pl.ds(0, 21)]), coming()
        own = {d: coming() for d in (2, 1, 3)}
        for d in own:
            send(shard(0), shard(0), zc(d), out, own[d])
        send(shard(0), shard(0), sib, out, across)

        def pass_on(d):
            arrived(shard(-d), own[d])
            send(shard(-d), shard(-d), sib, out, across)

        yield
        pass_on(1)
        pass_on(3)
        yield
        pass_on(2)
        yield
        arrived(es[k].at[pl.ds(0, 12)], across)

    def weights_grad():
        for b in range(3):
            hi, lo = zip(*[split(bxt[c, b]) for c in range(2)])
            hi, lo = jnp.concatenate(hi, axis=0), jnp.concatenate(lo, axis=0)
            bz = dot(theta_t[...], hi) + dot(theta_t[...], lo)
            terms = bz[:T] * bgt[0, b] + bz[T:] * bgt[1, b]
            cols = slice(b * T, (b + 1) * T)
            gw_ref[:, cols] = jnp.sum(terms, axis=0, keepdims=True) / coefs(b)[1]

    def reduce_row(k):
        def to(h, a, b):
            return xy(a, b) if h == 0 else xy(b, a)

        def fetch(h, p, q):
            dx, dy = (p, q) if h == 0 else (q, p)
            return run[by_row[3, 2 * (((x + dx) % 4) * 4 + (y + dy) % 4) + h]]

        out, out2 = leaving(vs.at[k]), leaving(ws.at[k])
        one, two, three = [coming() for _ in range(3)]

        def halves(v):
            return v[: T // 2], v[T // 2 :]

        for h in range(2):
            for q in range(4):
                for u, v in enumerate(halves(fetch(h, 2, q))):
                    vs[k, h, 0, u, q] = v.astype(BF)
            for u, d in ((0, 1), (1, -1)):
                send(vs.at[k, h, 0, u], vr1.at[k, h, u], to(h, d, 0), out, one)
        for h in range(2):
            for q in range(4):
                up, down = halves(fetch(h, 1, q))
                vs[k, h, 1, 1, q] = down.astype(BF)
                vkeep[k, h, 1, q, : T // 2] = up
                up, down = halves(fetch(h, 3, q))
                vs[k, h, 2, 0, q] = up.astype(BF)
                vkeep[k, h, 1, q, T // 2 :] = down
            send(vs.at[k, h, 1, 1], vr2.at[k, h, 0, 1], to(h, 1, 0), out, two)
            send(vs.at[k, h, 2, 0], vr2.at[k, h, 1, 0], to(h, -1, 0), out, two)
        for h in range(2):
            for q in range(4):
                vkeep[k, h, 0, q] = fetch(h, 0, q)
        yield
        arrived(vr1.at[k], one)
        for h in range(2):
            for q in range(4):
                up, down = halves(vkeep[k, h, 1, q])
                vs[k, h, 1, 0, q] = (up + vr1[k, h, 0, q].astype(F32)).astype(BF)
                vs[k, h, 2, 1, q] = (down + vr1[k, h, 1, q].astype(F32)).astype(BF)
            send(vs.at[k, h, 1, 0], vr2.at[k, h, 0, 0], to(h, 1, 0), out, two)
            send(vs.at[k, h, 2, 1], vr2.at[k, h, 1, 1], to(h, -1, 0), out, two)
        yield
        arrived(vr2.at[k], two)
        for q in (1, 3, 2, 0):
            for h in range(2):
                total = vkeep[k, h, 0, q]
                for p in range(2):
                    total = total + jnp.concatenate(
                        [vr2[k, h, p, u, q].astype(F32) for u in range(2)], axis=0
                    )
                if q:
                    ws[k, h, q - 1] = total.astype(BF)
                    send(ws.at[k, h, q - 1], wr.at[k, h, q - 1], to(h, 0, q), out2, three)
                else:
                    vkeep[k, h, 0, 0] = total
        yield
        arrived(wr.at[k], three)
        for h in range(2):
            v = vkeep[k, h, 0, 0]
            for q in range(3):
                v = v + wr[k, h, q].astype(F32)
            rows = pl.ds(h * T, T)
            cols = pl.ds((k % 2) * T, T)
            v = v * scale[rows, :T]
            if k < 2:
                y_ref[rows, cols] = v
            else:
                gz_ref[rows, cols] = v.astype(BF)

    def sum_theta():
        nt = (((1,), (1,)), ((), ()))
        for w in range(2):
            acc = jnp.zeros((F, T), F32)
            for b in range(3):
                xs = [split(bxt[c, b]) for c in range(2)]
                xh, xl = [jnp.concatenate([p[m] for p in xs], axis=0) for m in range(2)]
                eh, el = split(bgt[w, b] * coefs(b)[0])
                for p, q in ((xh, eh), (xl, eh), (xh, el)):
                    acc = acc + lax.dot_general(p, q, nt, preferred_element_type=F32)
            gl[:, w * T : (w + 1) * T] = acc
        out = [leaving(gl.at[pl.ds(0, 224)]), leaving(gp1.at[pl.ds(0, 24)]), leaving(g3.at[pl.ds(0, 3)])]
        out += [leaving(go.at[pl.ds(0, 24)]), leaving(go.at[pl.ds(0, 224)])]
        into = [coming() for _ in range(5)]
        for d in range(1, 8):
            to = (i + d) % 8
            send(gl.at[pl.ds(32 * to, 32)], g1.at[d - 1], (to, j), out[0], into[0])
        yield
        arrived(g1, into[0])
        own = gl[pl.ds(32 * i, 32)]
        for d in range(7):
            own = own + g1[d]
        gp1[...] = own
        for d in near:
            send(gp1.at[pl.ds(8 * ((x + d) % 4), 8)], g2.at[d - 1], xy(d, 0), out[1], into[1])
        yield
        arrived(g2, into[1])
        g3[y] = gp1[pl.ds(8 * x, 8)] + g2[0] + g2[1] + g2[2]
        for d in near:
            send(g3.at[y], g3.at[y], xy(0, d), out[2], into[2])
        yield
        arrived(g3.at[pl.ds(0, 3)], into[2])
        rows = pl.ds(32 * i + 8 * x, 8)
        go[rows] = ((g3[0] + g3[1]) + g3[2]) + g3[3]
        for d in near:
            send(go.at[rows], go.at[rows], xy(d, 0), out[3], into[3])
        yield
        arrived(go.at[pl.ds(0, 24)], into[3])
        rows = pl.ds(32 * i, 32)
        for d in range(1, 8):
            send(go.at[rows], go.at[rows], ((i + d) % 8, j), out[4], into[4])
        yield
        arrived(go.at[pl.ds(0, 224)], into[4])
        gt_ref[...] = go[...]

    def step(gen):
        next(gen, None)

    def drain(gen):
        for _ in gen:
            pass

    row = [gather_row(k) for k in range(4)]
    col = [reduce_col(k) for k in range(4)]
    full = [gather_col(k) for k in range(4)]
    back = [reduce_row(k) for k in range(4)]
    theta = sum_theta()
    def tables():
        theta_t[...] = jnp.transpose(theta_ref[...].astype(F32)).astype(BF)
        tiles[SLOTS] = jnp.zeros((T, T), BF)
        run[0] = jnp.zeros((T, T), F32)

    step(row[0])
    step(row[0])
    step(row[0])
    step(row[1])
    prepare(g_ref, 2)
    tables()
    step(row[0])
    step(row[1])
    step(row[1])
    step(row[2])
    step(row[0])
    load.wait()
    forward(0, 0)
    forward(0, 1)
    step(col[0])
    step(row[1])
    step(col[0])
    step(row[2])
    step(row[2])
    step(row[3])
    step(row[1])
    forward(1, 0)
    forward(1, 1)
    step(col[1])
    step(row[2])
    step(col[0])
    step(col[1])
    step(full[0])
    step(row[3])
    step(row[3])
    step(row[2])
    forward(2, 0)
    forward(2, 1)
    step(col[2])
    step(row[3])
    step(col[1])
    step(col[2])
    step(full[1])
    step(row[3])
    forward(3, 0)
    forward(3, 1)
    step(col[3])
    step(full[0])
    step(full[0])
    step(col[3])
    step(full[0])
    backward(0, 0)
    backward(0, 1)
    step(back[0])
    step(col[2])
    step(full[2])
    step(full[1])
    step(full[1])
    step(full[1])
    backward(1, 0)
    step(back[0])
    step(col[3])
    step(theta)
    step(full[3])
    backward(1, 1)
    step(back[1])
    step(back[0])
    step(full[2])
    step(full[2])
    weights_grad()
    step(full[2])
    backward(2, 0)
    step(theta)
    step(back[1])
    backward(2, 1)
    step(back[2])
    step(theta)
    step(back[0])
    step(full[3])
    step(full[3])
    step(back[1])
    step(full[3])
    backward(3, 0)
    backward(3, 1)
    step(theta)
    step(back[3])
    step(back[2])
    step(back[1])
    step(theta)
    step(back[3])
    step(back[2])
    step(back[3])
    step(theta)
    step(back[2])
    step(back[3])
    for ref, n in sends:
        pltpu.make_async_copy(ref, ref, ssem.at[n]).wait()


def tail(ys_ref, gz_ref, gt_ref, gw_ref, theta_ref, y_out, gx_out, gt_out, gw_out):
    theta = theta_ref[...]
    ys = ys_ref[...]
    hi = ys.astype(BF)
    lo = (ys - hi.astype(F32)).astype(BF)
    y = jnp.dot(hi, theta, preferred_element_type=F32)
    y_out[...] = (y + jnp.dot(lo, theta, preferred_element_type=F32)).astype(BF)
    nt = (((1,), (1,)), ((), ()))
    gx_out[...] = lax.dot_general(gz_ref[...], theta, nt, preferred_element_type=F32).astype(BF)
    gt_out[...] = gt_ref[...]
    gw_out[...] = gw_ref[...]


def shards(
    features, grad_out, theta, tile_values, tile_rows, tile_cols, tile_count,
    vertex_degree, edge_weight, edge_degree,
):
    smem = pl.BlockSpec(memory_space=pltpu.SMEM)
    vmem = pl.BlockSpec(memory_space=pltpu.VMEM)
    hbm = pl.BlockSpec(memory_space=pl.ANY)
    v = pltpu.VMEM
    scratch = [
        v((SLOTS + 1, T, T), BF),
        v((GB + 1, T, T), F32),
        v((2 * T, F), F32),
        v((F, F), BF),
        *[v((VB, T, T), BF)] * 4,
        *[v((EB, T, T), BF)] * 4,
        v((4, 4, 3, T, T), BF),
        v((4, 4, 3, T, T), BF),
        v((4, 4, 3, T, T), F32),
        v((4, 3, 3, T, T), BF),
        v((4, 3, 3, T, T), BF),
        v((2, 3, T, T), F32),
        v((2, 3, T, T), F32),
        v((4, 2, 3, 2, 4, T // 2, T), BF),
        v((4, 2, 2, 4, T // 2, T), BF),
        v((4, 2, 2, 2, 4, T // 2, T), BF),
        v((4, 2, 2, 4, T, T), F32),
        v((4, 2, 3, T, T), BF),
        v((4, 2, 3, T, T), BF),
        v((F, F), F32),
        v((7, 32, F), F32),
        v((32, F), F32),
        v((3, 8, F), F32),
        v((4, 8, F), F32),
        v((F, F), F32),
        pltpu.SemaphoreType.DMA,
        pltpu.SemaphoreType.DMA((NSEND,)),
        pltpu.SemaphoreType.DMA((NRECV,)),
    ]
    table = jax.ShapeDtypeStruct((8, 384), jnp.int32)
    by_col, by_row = pl.pallas_call(
        order_tiles,
        out_shape=(table, table),
        in_specs=[smem, vmem, vmem],
        out_specs=[vmem] * 2,
        cost_estimate=pl.CostEstimate(flops=1_000_000, bytes_accessed=30_000, transcendentals=0),
    )(tile_count, tile_rows.reshape(1, SLOTS), tile_cols.reshape(1, SLOTS))
    ys, gz, gt, gw = pl.pallas_call(
        body,
        out_shape=(
            jax.ShapeDtypeStruct((2 * T, F), F32),
            jax.ShapeDtypeStruct((2 * T, F), BF),
            jax.ShapeDtypeStruct((F, F), F32),
            jax.ShapeDtypeStruct((1, 3 * T), F32),
        ),
        in_specs=[smem] * 2 + [vmem] * 3 + [hbm] + [vmem] * 3,
        out_specs=[vmem] * 4,
        scratch_shapes=scratch,
        compiler_params=pltpu.CompilerParams(
            collective_id=0, has_side_effects=True, vmem_limit_bytes=60 * 1024 * 1024
        ),
        cost_estimate=pl.CostEstimate(
            flops=20_000_000_000, bytes_accessed=10_000_000, transcendentals=0
        ),
    )(
        by_col, by_row, features, grad_out, theta, tile_values, vertex_degree.reshape(1, 2 * T),
        edge_weight, edge_degree,
    )
    return pl.pallas_call(
        tail,
        out_shape=(
            jax.ShapeDtypeStruct((2 * T, F), BF),
            jax.ShapeDtypeStruct((2 * T, F), BF),
            jax.ShapeDtypeStruct((F, F), F32),
            jax.ShapeDtypeStruct((1, 3 * T), F32),
        ),
        in_specs=[vmem] * 5,
        out_specs=[vmem] * 4,
        cost_estimate=pl.CostEstimate(flops=100_000_000, bytes_accessed=2_000_000, transcendentals=0),
    )(ys, gz, gt, gw, theta)


def solution(mesh):
    both = ("vrow", "ecol")
    in_specs = (
        P(both, None), P(both, None), P(), P(both, None, None), P(both), P(both), P(both),
        P(both), P("ecol", "vrow"), P("ecol", "vrow"),
    )
    out_specs = (P(both, None), P(both, None), P(), P("ecol", "vrow"))
    return jax.shard_map(shards, mesh=mesh, in_specs=in_specs, out_specs=out_specs, check_vma=False)
```

```python
import jax
import jax.numpy as jnp
from jax import lax
from jax.experimental import pallas as pl
from jax.experimental.pallas import tpu as pltpu
from jax.sharding import PartitionSpec as P

BF = jnp.bfloat16
F32 = jnp.float32
MESH = pl.DeviceIdType.MESH
T = 128
F = 256
VB = 32
EB = 24
SLOTS = 256
GF = (SLOTS + EB) // 2
GB = (SLOTS + VB) // 2
PARTS = 2
NSEND = 29
NRECV = 69


def plan(key, other, live, pad):
    n = SLOTS

    def iota(shape, dim):
        return lax.broadcasted_iota(jnp.int32, shape, dim)

    key_l = jnp.where(iota((n, n), 1) < live, jnp.broadcast_to(key, (n, n)), n)
    key_s = jnp.transpose(key_l)
    other_s = jnp.transpose(jnp.broadcast_to(other, (n, n)))
    t = iota((n, n), 0)
    same = jnp.where((key_s == key_l) & (iota((n, n), 1) < t), 1, 0)
    rank = jnp.sum(same, axis=1, keepdims=True)
    hit = jnp.where(key_s[:, :T] == iota((n, T), 1), 1, 0)
    count = jnp.sum(hit, axis=0, keepdims=True)
    half = (count + 1) >> 1
    upto = iota((T, T), 0) <= iota((T, T), 1)
    half_s = jnp.transpose(jnp.broadcast_to(half, (T, T)))
    end = jnp.sum(jnp.where(upto, half_s, 0), axis=0, keepdims=True)
    start = 2 * (end - half)
    place = jnp.sum(hit * start, axis=1, keepdims=True) + rank
    place = jnp.where(key_s[:, :1] < n, place, -1)
    at = place == iota((n, pad), 1)
    tile = jnp.sum(jnp.where(at, t[:, :1] - n, 0), axis=0, keepdims=True) + n
    panel = jnp.sum(jnp.where(at, other_s[:, :1], 0), axis=0, keepdims=True)
    more = jnp.where(rank > 0, 1, 0)
    keep = jnp.sum(jnp.where(place == 2 * iota((n, pad), 1), more, 0), axis=0, keepdims=True)
    last = jnp.where(count > 0, end, 0)
    last = jnp.concatenate([last, jnp.zeros((1, pad - T), jnp.int32)], axis=1)
    return jnp.concatenate([tile, panel, keep, last, jnp.zeros((4, pad), jnp.int32)], axis=0)


def body(
    count_ref, rows_ref, cols_ref,
    x_ref, g_ref, theta_ref, values_ref, vdeg_ref, ew_ref, ed_ref,
    y_ref, gz_ref, gt_ref, gw_ref,
    tiles, run, scale, theta_t, plans, by_col, by_row,
    pt_0, pt_1, pt_2, pt_3, e_0, e_1, e_2, e_3,
    sib_s, sib_r, mine, zs, zr, bxt, bgt, vs, vr1, vr2, vkeep, ws, wr,
    gl, g1, gp1, g2, g3, go,
    tsem, psem, ssem, rsem,
):
    pts, es = (pt_0, pt_1, pt_2, pt_3), (e_0, e_1, e_2, e_3)
    i = lax.axis_index("vrow")
    j = lax.axis_index("ecol")
    z, core = i // 2, i % 2
    x, y = j // 4, j % 4

    def zc(d, c=None):
        return (((z + d) % 4) * 2 + (core if c is None else c), j)

    def xy(dx, dy):
        return (i, ((x + dx) % 4) * 4 + (y + dy) % 4)

    sib = (z * 2 + 1 - core, j)

    barrier = pltpu.get_barrier_semaphore()
    peers = [((i + d) % 8, j) for d in range(1, 8)]
    peers += [xy(d, 0) for d in (1, 2, 3)] + [xy(0, d) for d in (1, 2, 3)]
    for p in peers:
        pl.semaphore_signal(barrier, inc=1, device_id=p, device_id_type=MESH)

    load = pltpu.make_async_copy(values_ref, tiles.at[pl.ds(0, SLOTS)], tsem)
    load.start()

    deg = vdeg_ref[...].astype(F32)
    scale[...] = jnp.transpose(jnp.broadcast_to(1.0 / jnp.sqrt(deg), (F, 2 * T)))

    def prepare(src, k):
        part = jnp.transpose(src[...].astype(F32) * scale[...]).astype(BF)
        for c in range(2):
            for h in range(2):
                pts[k + c][2 * j + h] = part[c * T : (c + 1) * T, h * T : (h + 1) * T]

    prepare(x_ref, 0)
    pl.semaphore_wait(barrier, len(peers))

    sends, groups = [], [0, 0]

    def send(src, dst, to, out, into):
        pltpu.make_async_remote_copy(
            src_ref=src, dst_ref=dst, send_sem=ssem.at[out], recv_sem=rsem.at[into],
            device_id=to, device_id_type=MESH,
        ).start()

    def leaving(ref):
        n = groups[0]
        groups[0] += 1
        sends.append((ref, n))
        return n

    def coming():
        groups[1] += 1
        return groups[1] - 1

    def arrived(ref, n):
        pltpu.make_async_copy(ref, ref, rsem.at[n]).wait()

    near = (1, 3, 2)

    def gather_row(k):
        pt = pts[k]

        def to(h, a, b):
            return xy(b, a) if h == 0 else xy(a, b)

        def block(h, a, b):
            dx, dy = (b, a) if h == 0 else (a, b)
            return pt.at[2 * (((x + dx) % 4) * 4 + (y + dy) % 4) + h]

        out = leaving(pt.at[pl.ds(0, 30)])
        one, two, three, four = [coming() for _ in range(4)]
        for d in near:
            for h in range(2):
                send(block(h, 0, 0), block(h, 0, 0), to(h, d, 0), out, one)

        def across(a, into):
            for d in (1, -1):
                for h in range(2):
                    send(block(h, a, 0), block(h, a, 0), to(h, 0, d), out, into)

        def onward(a):
            for d, start in ((1, 0), (-1, T // 2)):
                for h in range(2):
                    r = block(h, a, -d).at[pl.ds(start, T // 2)]
                    send(r, r, to(h, 0, d), out, four)

        across(0, two)
        yield
        arrived(pt.at[pl.ds(0, 6)], one)
        for a in near:
            across(a, three)
        yield
        arrived(pt.at[pl.ds(0, 4)], two)
        onward(0)
        yield
        arrived(pt.at[pl.ds(0, 12)], three)
        for a in near:
            onward(a)
        yield
        arrived(pt.at[pl.ds(0, 8)], four)

    def sweep(table, groups, unit, part, product):
        per = groups // PARTS

        def turn(n, acc):
            for u in range(unit):
                g = part * per + n * unit + u
                acc = product(2 * g) + table[2, g].astype(F32) * acc
                run[g + 1] = acc
            return acc

        lax.fori_loop(0, per // unit, turn, run[part * per])

    def dot(a, b):
        return jnp.dot(a, b, preferred_element_type=F32)

    def forward(k, part):
        pt = pts[k]

        def product(s):
            lhs = jnp.concatenate([pt[by_col[1, s]], pt[by_col[1, s + 1]]], axis=1)
            rhs = jnp.concatenate([tiles[by_col[0, s]], tiles[by_col[0, s + 1]]], axis=0)
            return dot(lhs, rhs)

        sweep(by_col, GF, 35, part, product)

    def backward(k, part):
        e = es[k]

        def product(s):
            lhs = jnp.concatenate([tiles[by_row[0, s]], tiles[by_row[0, s + 1]]], axis=1)
            rhs = jnp.concatenate([e[by_row[1, s]], e[by_row[1, s + 1]]], axis=0)
            return dot(lhs, rhs)

        sweep(by_row, GB, 36, part, product)

    def split(value):
        hi = value.astype(BF)
        return hi, (value - hi.astype(F32)).astype(BF)

    def coefs(b):
        cols = slice(b * T, (b + 1) * T)
        d = ed_ref[:, cols].astype(F32)
        return ew_ref[:, cols] / d, d

    def reduce_col(k):
        order = (2, 1, 3, 0)
        out, out2 = leaving(sib_s.at[k]), leaving(zs.at[k])
        pair, into = [coming() for _ in range(4)], coming()
        for d in order:
            zd = (z + d) % 4
            for b in range(3):
                sib_s[k, d, b] = run[by_col[3, 3 * (2 * zd + 1 - core) + b]].astype(BF)
            send(sib_s.at[k, d], sib_r.at[k, d], sib, out, pair[d])
        for d in order:
            zd = (z + d) % 4
            for b in range(3):
                mine[k, d, b] = run[by_col[3, 3 * (2 * zd + core) + b]]
        yield
        for d in order:
            arrived(sib_r.at[k, d], pair[d])
            for b in range(3):
                total = mine[k, d, b] + sib_r[k, d, b].astype(F32)
                if d == 0:
                    mine[k, 0, b] = total
                else:
                    zs[k, d - 1, b] = total.astype(BF)
            if d:
                send(zs.at[k, d - 1], zr.at[k, d - 1], zc(d), out2, into)
        yield
        arrived(zr.at[k], into)
        for b in range(3):
            total = mine[k, 0, b]
            for d in (1, 2, 3):
                total = total + zr[k, d - 1, b].astype(F32)
            if k < 2:
                bxt[k, b] = total
            else:
                bgt[k - 2, b] = total
            es[k][3 * i + b] = jnp.transpose(total * coefs(b)[0]).astype(BF)

    def gather_col(k):
        def shard(d):
            return es[k].at[pl.ds(3 * (2 * ((z + d) % 4) + core), 3)]

        out, across = leaving(es[k].at[pl.ds(0, 21)]), coming()
        own = {d: coming() for d in (2, 1, 3)}
        for d in own:
            send(shard(0), shard(0), zc(d), out, own[d])
        send(shard(0), shard(0), sib, out, across)

        def pass_on(d):
            arrived(shard(-d), own[d])
            send(shard(-d), shard(-d), sib, out, across)

        yield
        pass_on(1)
        pass_on(3)
        yield
        pass_on(2)
        yield
        arrived(es[k].at[pl.ds(0, 12)], across)

    def weights_grad():
        for b in range(3):
            hi, lo = zip(*[split(bxt[c, b]) for c in range(2)])
            hi, lo = jnp.concatenate(hi, axis=0), jnp.concatenate(lo, axis=0)
            bz = dot(theta_t[...], hi) + dot(theta_t[...], lo)
            terms = bz[:T] * bgt[0, b] + bz[T:] * bgt[1, b]
            cols = slice(b * T, (b + 1) * T)
            gw_ref[:, cols] = jnp.sum(terms, axis=0, keepdims=True) / coefs(b)[1]

    def reduce_row(k):
        def to(h, a, b):
            return xy(a, b) if h == 0 else xy(b, a)

        def fetch(h, p, q):
            dx, dy = (p, q) if h == 0 else (q, p)
            return run[by_row[3, 2 * (((x + dx) % 4) * 4 + (y + dy) % 4) + h]]

        out, out2 = leaving(vs.at[k]), leaving(ws.at[k])
        one, two, three = [coming() for _ in range(3)]

        def halves(v):
            return v[: T // 2], v[T // 2 :]

        for h in range(2):
            for q in range(4):
                for u, v in enumerate(halves(fetch(h, 2, q))):
                    vs[k, h, 0, u, q] = v.astype(BF)
            for u, d in ((0, 1), (1, -1)):
                send(vs.at[k, h, 0, u], vr1.at[k, h, u], to(h, d, 0), out, one)
        for h in range(2):
            for q in range(4):
                up, down = halves(fetch(h, 1, q))
                vs[k, h, 1, 1, q] = down.astype(BF)
                vkeep[k, h, 1, q, : T // 2] = up
                up, down = halves(fetch(h, 3, q))
                vs[k, h, 2, 0, q] = up.astype(BF)
                vkeep[k, h, 1, q, T // 2 :] = down
            send(vs.at[k, h, 1, 1], vr2.at[k, h, 0, 1], to(h, 1, 0), out, two)
            send(vs.at[k, h, 2, 0], vr2.at[k, h, 1, 0], to(h, -1, 0), out, two)
        for h in range(2):
            for q in range(4):
                vkeep[k, h, 0, q] = fetch(h, 0, q)
        yield
        arrived(vr1.at[k], one)
        for h in range(2):
            for q in range(4):
                up, down = halves(vkeep[k, h, 1, q])
                vs[k, h, 1, 0, q] = (up + vr1[k, h, 0, q].astype(F32)).astype(BF)
                vs[k, h, 2, 1, q] = (down + vr1[k, h, 1, q].astype(F32)).astype(BF)
            send(vs.at[k, h, 1, 0], vr2.at[k, h, 0, 0], to(h, 1, 0), out, two)
            send(vs.at[k, h, 2, 1], vr2.at[k, h, 1, 1], to(h, -1, 0), out, two)
        yield
        arrived(vr2.at[k], two)
        for q in (1, 3, 2, 0):
            for h in range(2):
                total = vkeep[k, h, 0, q]
                for p in range(2):
                    total = total + jnp.concatenate(
                        [vr2[k, h, p, u, q].astype(F32) for u in range(2)], axis=0
                    )
                if q:
                    ws[k, h, q - 1] = total.astype(BF)
                    send(ws.at[k, h, q - 1], wr.at[k, h, q - 1], to(h, 0, q), out2, three)
                else:
                    vkeep[k, h, 0, 0] = total
        yield
        arrived(wr.at[k], three)
        for h in range(2):
            v = vkeep[k, h, 0, 0]
            for q in range(3):
                v = v + wr[k, h, q].astype(F32)
            rows = pl.ds(h * T, T)
            cols = pl.ds((k % 2) * T, T)
            v = v * scale[rows, :T]
            if k < 2:
                y_ref[rows, cols] = v
            else:
                gz_ref[rows, cols] = v.astype(BF)

    def sum_theta():
        nt = (((1,), (1,)), ((), ()))
        for w in range(2):
            acc = jnp.zeros((F, T), F32)
            for b in range(3):
                xs = [split(bxt[c, b]) for c in range(2)]
                xh, xl = [jnp.concatenate([p[m] for p in xs], axis=0) for m in range(2)]
                eh, el = split(bgt[w, b] * coefs(b)[0])
                for p, q in ((xh, eh), (xl, eh), (xh, el)):
                    acc = acc + lax.dot_general(p, q, nt, preferred_element_type=F32)
            gl[:, w * T : (w + 1) * T] = acc
        out = [leaving(gl.at[pl.ds(0, 224)]), leaving(gp1.at[pl.ds(0, 24)]), leaving(g3.at[pl.ds(0, 3)])]
        out += [leaving(go.at[pl.ds(0, 24)]), leaving(go.at[pl.ds(0, 224)])]
        into = [coming() for _ in range(5)]
        for d in range(1, 8):
            to = (i + d) % 8
            send(gl.at[pl.ds(32 * to, 32)], g1.at[d - 1], (to, j), out[0], into[0])
        yield
        arrived(g1, into[0])
        own = gl[pl.ds(32 * i, 32)]
        for d in range(7):
            own = own + g1[d]
        gp1[...] = own
        for d in near:
            send(gp1.at[pl.ds(8 * ((x + d) % 4), 8)], g2.at[d - 1], xy(d, 0), out[1], into[1])
        yield
        arrived(g2, into[1])
        g3[y] = gp1[pl.ds(8 * x, 8)] + g2[0] + g2[1] + g2[2]
        for d in near:
            send(g3.at[y], g3.at[y], xy(0, d), out[2], into[2])
        yield
        arrived(g3.at[pl.ds(0, 3)], into[2])
        rows = pl.ds(32 * i + 8 * x, 8)
        go[rows] = ((g3[0] + g3[1]) + g3[2]) + g3[3]
        for d in near:
            send(go.at[rows], go.at[rows], xy(d, 0), out[3], into[3])
        yield
        arrived(go.at[pl.ds(0, 24)], into[3])
        rows = pl.ds(32 * i, 32)
        for d in range(1, 8):
            send(go.at[rows], go.at[rows], ((i + d) % 8, j), out[4], into[4])
        yield
        arrived(go.at[pl.ds(0, 224)], into[4])
        gt_ref[...] = go[...]

    def step(gen):
        next(gen, None)

    def drain(gen):
        for _ in gen:
            pass

    row = [gather_row(k) for k in range(4)]
    col = [reduce_col(k) for k in range(4)]
    full = [gather_col(k) for k in range(4)]
    back = [reduce_row(k) for k in range(4)]
    theta = sum_theta()
    copies = [
        pltpu.make_async_copy(plans.at[m], dst, psem.at[m])
        for m, dst in enumerate((by_col, by_row))
    ]

    def tables():
        live = count_ref[0]
        plans[0] = plan(cols_ref[...], rows_ref[...], live, 384)
        plans[1] = plan(rows_ref[...], cols_ref[...], live, 384)
        for c in copies:
            c.start()
        theta_t[...] = jnp.transpose(theta_ref[...].astype(F32)).astype(BF)
        tiles[SLOTS] = jnp.zeros((T, T), BF)
        run[0] = jnp.zeros((T, T), F32)

    step(row[0])
    step(row[0])
    step(row[0])
    step(row[1])
    prepare(g_ref, 2)
    tables()
    step(row[0])
    step(row[1])
    step(row[1])
    step(row[2])
    step(row[0])
    load.wait()
    for c in copies:
        c.wait()
    forward(0, 0)
    forward(0, 1)
    step(col[0])
    step(row[1])
    step(col[0])
    step(row[2])
    step(row[2])
    step(row[3])
    step(row[1])
    forward(1, 0)
    forward(1, 1)
    step(col[1])
    step(row[2])
    step(col[0])
    step(col[1])
    step(full[0])
    step(row[3])
    step(row[3])
    step(row[2])
    forward(2, 0)
    forward(2, 1)
    step(col[2])
    step(row[3])
    step(col[1])
    step(col[2])
    step(full[1])
    step(row[3])
    forward(3, 0)
    forward(3, 1)
    step(col[3])
    step(full[0])
    step(full[0])
    step(col[3])
    step(full[0])
    backward(0, 0)
    backward(0, 1)
    step(back[0])
    step(col[2])
    step(full[2])
    step(full[1])
    step(full[1])
    step(full[1])
    backward(1, 0)
    step(back[0])
    step(col[3])
    step(theta)
    step(full[3])
    backward(1, 1)
    step(back[1])
    step(back[0])
    step(full[2])
    step(full[2])
    weights_grad()
    step(full[2])
    backward(2, 0)
    step(theta)
    step(back[1])
    backward(2, 1)
    step(back[2])
    step(theta)
    step(back[0])
    step(full[3])
    step(full[3])
    step(back[1])
    step(full[3])
    backward(3, 0)
    backward(3, 1)
    step(theta)
    step(back[3])
    step(back[2])
    step(back[1])
    step(theta)
    step(back[3])
    step(back[2])
    step(back[3])
    step(theta)
    step(back[2])
    step(back[3])
    for ref, n in sends:
        pltpu.make_async_copy(ref, ref, ssem.at[n]).wait()


def tail(ys_ref, gz_ref, gt_ref, gw_ref, theta_ref, y_out, gx_out, gt_out, gw_out):
    theta = theta_ref[...]
    ys = ys_ref[...]
    hi = ys.astype(BF)
    lo = (ys - hi.astype(F32)).astype(BF)
    y = jnp.dot(hi, theta, preferred_element_type=F32)
    y_out[...] = (y + jnp.dot(lo, theta, preferred_element_type=F32)).astype(BF)
    nt = (((1,), (1,)), ((), ()))
    gx_out[...] = lax.dot_general(gz_ref[...], theta, nt, preferred_element_type=F32).astype(BF)
    gt_out[...] = gt_ref[...]
    gw_out[...] = gw_ref[...]


def shards(
    features, grad_out, theta, tile_values, tile_rows, tile_cols, tile_count,
    vertex_degree, edge_weight, edge_degree,
):
    smem = pl.BlockSpec(memory_space=pltpu.SMEM)
    vmem = pl.BlockSpec(memory_space=pltpu.VMEM)
    hbm = pl.BlockSpec(memory_space=pl.ANY)
    v = pltpu.VMEM
    scratch = [
        v((SLOTS + 1, T, T), BF),
        v((GB + 1, T, T), F32),
        v((2 * T, F), F32),
        v((F, F), BF),
        v((2, 8, 384), jnp.int32),
        pltpu.SMEM((8, 384), jnp.int32),
        pltpu.SMEM((8, 384), jnp.int32),
        *[v((VB, T, T), BF)] * 4,
        *[v((EB, T, T), BF)] * 4,
        v((4, 4, 3, T, T), BF),
        v((4, 4, 3, T, T), BF),
        v((4, 4, 3, T, T), F32),
        v((4, 3, 3, T, T), BF),
        v((4, 3, 3, T, T), BF),
        v((2, 3, T, T), F32),
        v((2, 3, T, T), F32),
        v((4, 2, 3, 2, 4, T // 2, T), BF),
        v((4, 2, 2, 4, T // 2, T), BF),
        v((4, 2, 2, 2, 4, T // 2, T), BF),
        v((4, 2, 2, 4, T, T), F32),
        v((4, 2, 3, T, T), BF),
        v((4, 2, 3, T, T), BF),
        v((F, F), F32),
        v((7, 32, F), F32),
        v((32, F), F32),
        v((3, 8, F), F32),
        v((4, 8, F), F32),
        v((F, F), F32),
        pltpu.SemaphoreType.DMA,
        pltpu.SemaphoreType.DMA((2,)),
        pltpu.SemaphoreType.DMA((NSEND,)),
        pltpu.SemaphoreType.DMA((NRECV,)),
    ]
    ys, gz, gt, gw = pl.pallas_call(
        body,
        out_shape=(
            jax.ShapeDtypeStruct((2 * T, F), F32),
            jax.ShapeDtypeStruct((2 * T, F), BF),
            jax.ShapeDtypeStruct((F, F), F32),
            jax.ShapeDtypeStruct((1, 3 * T), F32),
        ),
        in_specs=[smem] + [vmem] * 5 + [hbm] + [vmem] * 3,
        out_specs=[vmem] * 4,
        scratch_shapes=scratch,
        compiler_params=pltpu.CompilerParams(
            collective_id=0, has_side_effects=True, vmem_limit_bytes=60 * 1024 * 1024
        ),
        cost_estimate=pl.CostEstimate(
            flops=20_000_000_000, bytes_accessed=10_000_000, transcendentals=0
        ),
    )(
        tile_count, tile_rows.reshape(1, SLOTS), tile_cols.reshape(1, SLOTS), features, grad_out,
        theta, tile_values, vertex_degree.reshape(1, 2 * T), edge_weight, edge_degree,
    )
    return pl.pallas_call(
        tail,
        out_shape=(
            jax.ShapeDtypeStruct((2 * T, F), BF),
            jax.ShapeDtypeStruct((2 * T, F), BF),
            jax.ShapeDtypeStruct((F, F), F32),
            jax.ShapeDtypeStruct((1, 3 * T), F32),
        ),
        in_specs=[vmem] * 5,
        out_specs=[vmem] * 4,
        cost_estimate=pl.CostEstimate(flops=100_000_000, bytes_accessed=2_000_000, transcendentals=0),
    )(ys, gz, gt, gw, theta)


def solution(mesh):
    both = ("vrow", "ecol")
    in_specs = (
        P(both, None), P(both, None), P(), P(both, None, None), P(both), P(both), P(both),
        P(both), P("ecol", "vrow"), P("ecol", "vrow"),
    )
    out_specs = (P(both, None), P(both, None), P(), P("ecol", "vrow"))
    return jax.shard_map(shards, mesh=mesh, in_specs=in_specs, out_specs=out_specs, check_vma=False)
```
